256 devices in a mesh: member: 16 (over z, core), domain: 16 (over x, y).
Axes of the slice: x: 4, y: 4, z: 8, core: 2. Of those that a mesh axis runs over, the one named last changes fastest.
Arguments:
- state: bfloat16 [256, 8, 256, 512], P('member', None, 'domain'), may hold values from -6 to 6
- spreading_number: float32 [256, 512], P('domain'), may hold values from 0.04 to 0.2
- zonal_transport_number: float32 [256, 512], P('domain'), may hold values from -0.5 to 0.5
- meridional_transport_number: float32 [256, 512], P('domain'), may hold values from -0.5 to 0.5
- obs_count: int32 [256, 4], P(('domain', 'member')), may hold values from 16 to 128, as said below
- obs_index: int32 [256, 4, 128], P(('domain', 'member')), may hold values from 0 to 1023
- obs_value: float32 [256, 4, 128], P(('domain', 'member')), may hold values from -6 to 6
- obs_weight: float32 [256, 4, 128], P(('domain', 'member')), may hold values from 0.25 to 4
Outputs:
- analysis: bfloat16 [256, 8, 256, 512], P('member', None, 'domain')
The draws below stay inside these ranges and needn't reach their ends.
Inputs may be any that keep to these rules, and one draw needn't show every extreme that they name: `obs_count`: each latitude row has at least one patch with exactly 128 observations.
All inputs are finite; a program needn't handle non-finite values.
Results may differ from the reference program's by a relative error of at most 0.0067.
Values may be sent and summed in bfloat16 or wider, within the bound.
No kernel may reach another device: no remote copies, remote signals or barrier semaphores. Data moves between devices by JAX's collectives and lax.ppermute only.
A program may use at most 64 MiB of HBM per device.

```python
import math
import jax
import jax.numpy as jnp
from jax import lax

F = 8
LEV = 1
MEM_DEV = 16
PC = 128
OBS_MAX = 128
ITERS = 6
PATCH_ROW = 4
TRAJECTORY_COUNT = 256
PARALLEL_COUNT = 256
MERIDIAN_COUNT = 512


def draw_obs_count(key, part):
    key = jax.random.fold_in(key, 11)
    key_counts, key_full = jax.random.split(key)
    counts = jax.random.randint(key_counts, (PARALLEL_COUNT, PATCH_ROW), OBS_MAX // 8, OBS_MAX + 1)
    full_col = jax.random.randint(key_full, (PARALLEL_COUNT, 1), 0, PATCH_ROW)
    columns = jnp.arange(PATCH_ROW, dtype=jnp.int32)[None, :]
    return jnp.where(columns == full_col, OBS_MAX, counts).astype(jnp.int32)


def touch_ends(array, stream_key, smallest, high):
    shape = array.shape
    index_at = [jax.random.randint(jax.random.fold_in(stream_key, axis), (), 0, shape[axis]) for axis in range(len(shape))]
    array = array.at[tuple(index_at)].set(smallest)
    longest = shape.index(max(shape))
    index_at[longest] = (index_at[longest] + 1) % shape[longest]
    return array.at[tuple(index_at)].set(high)


def shard_levels(own_key, extent, cuts, smallest, top_value):
    def one(dim, shards_of):
        draws = jax.random.uniform(jax.random.fold_in(jax.random.fold_in(own_key, 6), dim), (shards_of,), jnp.float32, smallest / len(cuts), top_value / len(cuts))
        return jnp.repeat(jnp.exp(draws), extent[dim] // shards_of).reshape((-1,) + (1,) * (len(extent) - dim - 1))

    level = one(*cuts[0])
    for cut in cuts[1:]:
        level = level * one(*cut)
    return level


def normal_values(key, extent, width, reach, shards=(), kind=jnp.bfloat16):
    loudness = shard_levels(key, extent, shards, -0.22, 0.18) if shards else 1.0
    array = jax.random.normal(key, extent, jnp.float32) * width * loudness
    return jnp.minimum(jnp.maximum(array, -reach), reach).astype(kind)


def setup_inputs(seed: int = 0) -> dict:
    keys = jax.random.split(jax.random.key(seed), 9)
    return {
        "state": normal_values(keys[0], (TRAJECTORY_COUNT, F * LEV, PARALLEL_COUNT, MERIDIAN_COUNT), 1.0, 6.0, ((0, 16), (2, 16))),
        "spreading_number": jnp.clip(jnp.exp(math.log(0.2) - 1.609438 * jax.random.uniform(keys[1], (PARALLEL_COUNT, MERIDIAN_COUNT), jnp.float32) ** shard_levels(keys[1], (PARALLEL_COUNT, MERIDIAN_COUNT), ((0, 16),), -0.2, 0.2)), 0.04, 0.2),
        "zonal_transport_number": jnp.clip(jax.random.uniform(keys[2], (PARALLEL_COUNT, MERIDIAN_COUNT), jnp.float32, -0.5, 0.5) * shard_levels(keys[2], (PARALLEL_COUNT, MERIDIAN_COUNT), ((0, 16),), -0.4, 0.0), -0.5, 0.5),
        "meridional_transport_number": jnp.clip(jax.random.uniform(keys[3], (PARALLEL_COUNT, MERIDIAN_COUNT), jnp.float32, -0.5, 0.5) * shard_levels(keys[3], (PARALLEL_COUNT, MERIDIAN_COUNT), ((0, 16),), -0.4, 0.0), -0.5, 0.5),
        "obs_count": draw_obs_count(jax.random.fold_in(keys[8], 71), 0),
        "obs_index": touch_ends(jax.random.randint(keys[5], (PARALLEL_COUNT, PATCH_ROW, OBS_MAX), 0, F * LEV * PC), jax.random.fold_in(keys[5], 1), 0, (F * LEV * PC) - 1).astype(jnp.int32),
        "obs_value": normal_values(keys[6], (PARALLEL_COUNT, PATCH_ROW, OBS_MAX), 1.0, 6.0, ((0, 256),), jnp.float32),
        "obs_weight": jnp.clip(jnp.exp(math.log(4.0) - 2.7725887 * jax.random.uniform(keys[7], (PARALLEL_COUNT, PATCH_ROW, OBS_MAX), jnp.float32) ** shard_levels(keys[7], (PARALLEL_COUNT, PATCH_ROW, OBS_MAX), ((0, 256),), -0.2, 0.2)), 0.25, 4.0),
    }


def advance(extended, spreading_number, zonal_transport_number, meridional_transport_number):
    centre = extended[:, :, 1:-1]
    north_rows = extended[:, :, 2:]
    south_rows = extended[:, :, :-2]
    east_cols = jnp.roll(centre, -1, axis=3)
    west_cols = jnp.roll(centre, 1, axis=3)
    laplace_term = east_cols + west_cols + north_rows + south_rows - 4.0 * centre
    return centre + spreading_number * laplace_term - 0.5 * zonal_transport_number * (east_cols - west_cols) - 0.5 * meridional_transport_number * (north_rows - south_rows)

def pad_rows(field):
    return jnp.pad(field, ((0, 0), (0, 0), (1, 1), (0, 0)))

def predict_trajectory_batch(trajectory_sequence, spreading_number, zonal_transport_number, meridional_transport_number):
    middle = advance(pad_rows(trajectory_sequence.astype(jnp.float32)), spreading_number, zonal_transport_number, meridional_transport_number).astype(jnp.bfloat16)
    middle = lax.optimization_barrier(middle)
    return advance(pad_rows(middle.astype(jnp.float32)), spreading_number, zonal_transport_number, meridional_transport_number).astype(jnp.bfloat16)

def analyse(patch_state, obs_count, obs_index, obs_value, obs_weight):
    trajectory_sequence, variable_names, patches, cells = patch_state.shape
    slots = obs_index.shape[1]
    highest = lax.Precision.HIGHEST
    values = patch_state.astype(jnp.float32)
    centre = lax.optimization_barrier(jnp.mean(values, axis=0))
    pert = (values - centre).astype(jnp.bfloat16)
    flat = jnp.transpose(values, (2, 0, 1, 3)).reshape(patches, trajectory_sequence, variable_names * cells)
    picked = jnp.broadcast_to(obs_index[:, None, :], (patches, trajectory_sequence, slots))
    observed = jnp.take_along_axis(flat, picked, axis=2)
    obs_mean = lax.optimization_barrier(jnp.mean(observed, axis=1))
    obs_pert = observed - obs_mean[:, None, :]
    live = (jnp.arange(slots, dtype=jnp.int32)[None, :] < obs_count[:, None]).astype(jnp.float32)
    precision_w = obs_weight * live
    innov = obs_value - obs_mean
    identity = jnp.eye(trajectory_sequence, dtype=jnp.float32)
    system = jnp.einsum('pko,pjo->pkj', obs_pert * precision_w[:, None, :], obs_pert, precision=highest) + (trajectory_sequence - 1) * identity
    scale = jnp.sqrt(lax.optimization_barrier(jnp.sum(system * system, axis=(1, 2))))
    iterate = system / scale[:, None, None]
    inverse = jnp.broadcast_to(identity, system.shape)
    for sweep_no in range(ITERS):
        factor = 1.5 * identity - 0.5 * jnp.matmul(inverse, iterate, precision=highest)
        iterate = jnp.matmul(iterate, factor, precision=highest)
        inverse = jnp.matmul(factor, inverse, precision=highest)
    root_inv = inverse / jnp.sqrt(scale)[:, None, None]
    project = jnp.einsum('pko,po->pk', obs_pert, precision_w * innov, precision=highest)
    halfway = jnp.einsum('pkj,pj->pk', root_inv, project, precision=highest)
    wmean = jnp.einsum('pkj,pj->pk', root_inv, halfway, precision=highest)
    weights = (math.sqrt(trajectory_sequence - 1) * root_inv + wmean[:, :, None]).astype(jnp.bfloat16)
    analysed = jnp.einsum('kcpx,pkj->jcpx', pert.astype(jnp.float32), weights.astype(jnp.float32)) + centre[None]
    return analysed.astype(jnp.bfloat16)

def reference(state, spreading_number, zonal_transport_number, meridional_transport_number, obs_count, obs_index, obs_value, obs_weight):
    variable_names = F * LEV
    trajectory_batches = state.reshape(TRAJECTORY_COUNT // MEM_DEV, MEM_DEV, variable_names, PARALLEL_COUNT, MERIDIAN_COUNT)
    predict_advance_once = lax.map(lambda trajectory_sequence: predict_trajectory_batch(trajectory_sequence, spreading_number, zonal_transport_number, meridional_transport_number), trajectory_batches)
    predict_advance_once = predict_advance_once.reshape(TRAJECTORY_COUNT, variable_names, PARALLEL_COUNT, MERIDIAN_COUNT)

    def one_row(parallel_position):
        zonal_strip = lax.dynamic_index_in_dim(predict_advance_once, parallel_position, axis=2, keepdims=False)
        patch_state = zonal_strip.reshape(TRAJECTORY_COUNT, variable_names, PATCH_ROW, PC)
        result = analyse(patch_state, obs_count[parallel_position], obs_index[parallel_position], obs_value[parallel_position], obs_weight[parallel_position])
        return result.reshape(TRAJECTORY_COUNT, variable_names, MERIDIAN_COUNT)
    rows_done = lax.map(one_row, jnp.arange(PARALLEL_COUNT, dtype=jnp.int32))
    return jnp.transpose(rows_done, (1, 2, 0, 3))
```

```python
import math

import jax
import jax.numpy as jnp
from jax import lax
from jax.experimental import pallas as pl
from jax.experimental.pallas import tpu as pltpu
from jax.sharding import PartitionSpec as P

ITERS = 6
F32 = jnp.float32
BF16 = jnp.bfloat16


def halves(x):
    high = x.astype(BF16)
    return high, (x - high.astype(F32)).astype(BF16)


def thirds(x):
    high = x.astype(BF16)
    rest = x - high.astype(F32)
    mid = rest.astype(BF16)
    return high, mid, (rest - mid.astype(F32)).astype(BF16)


def dot(a, b):
    return jnp.dot(a, b, preferred_element_type=F32)


def row_picker(rows, first_row, span, members):
    out = lax.broadcasted_iota(jnp.int32, (rows * members, members * span), 0)
    src = lax.broadcasted_iota(jnp.int32, (rows * members, members * span), 1)
    row = out // members + first_row
    member = out % members
    return (src == member * span + row).astype(F32).astype(BF16)


def edges_kernel(state_ref, s_ref, z_ref, m_ref, south_ref, north_ref):
    field = pl.program_id(0)
    flat = state_ref[:, 0].reshape(256, 512)
    low = dot(row_picker(2, 0, 16, 16), flat).astype(BF16).reshape(2, 16, 512)
    high = dot(row_picker(2, 14, 16, 16), flat).astype(BF16).reshape(2, 16, 512)
    north_ref[pl.ds(2 * field, 2)] = high
    south_ref[pl.ds(2 * field, 2)] = low

    @pl.when(field == 0)
    def _():
        for out_ref, row in ((south_ref, 0), (north_ref, 15)):
            parts = []
            for ref in (s_ref, z_ref, m_ref):
                parts += list(thirds(ref[row : row + 1]))
            parts.append(jnp.zeros((7, 512), BF16))
            out_ref[16] = jnp.concatenate(parts, axis=0)


def edges(state, s, z, m):
    whole = pl.BlockSpec((16, 512), lambda f: (0, 0))
    shape = jax.ShapeDtypeStruct((17, 16, 512), BF16)
    out = pl.BlockSpec((17, 16, 512), lambda f: (0, 0, 0))
    return pl.pallas_call(
        edges_kernel,
        grid=(8,),
        in_specs=[pl.BlockSpec((16, 1, 16, 512), lambda f: (0, f, 0, 0)), whole, whole, whole],
        out_specs=[out, out],
        out_shape=[shape, shape],
        name="edges",
    )(state, s, z, m)


def coefficients(s, z, m):
    return (
        1.0 - 4.0 * s,
        s - 0.5 * z,
        s + 0.5 * z,
        s - 0.5 * m,
        s + 0.5 * m,
    )


def step_row(centre, north, south, coef):
    east = pltpu.roll(centre, 511, 1)
    west = pltpu.roll(centre, 1, 1)
    c, e, w, n, so = coef
    return centre * c + east * e + west * w + north * n + south * so


def forecast_kernel(
    flags_ref, state_ref, s_ref, z_ref, m_ref, low_ref, high_ref, out_ref, pick, coef, field_rows, middle
):
    field = pl.program_id(0)

    @pl.when(field == 0)
    def _():
        pick[...] = row_picker(16, 0, 16, 16)

        def put(row, s, z, m):
            for k, value in enumerate(coefficients(s, z, m)):
                coef[k, row] = jnp.broadcast_to(value, (8, 512))

        for ref, row in ((low_ref, 0), (high_ref, 17)):
            part = ref[16].astype(F32)
            rows = [part[3 * k : 3 * k + 1] + part[3 * k + 1 : 3 * k + 2] + part[3 * k + 2 : 3 * k + 3] for k in range(3)]
            put(row, *rows)
        for row in range(16):
            put(row + 1, s_ref[row : row + 1], z_ref[row : row + 1], m_ref[row : row + 1])

    flat = state_ref[:, 0].reshape(256, 512)
    field_rows[2:18] = dot(pick[...], flat).reshape(16, 16, 512)
    field_rows[0:2] = low_ref[pl.ds(2 * field, 2)].astype(F32)
    field_rows[18:20] = high_ref[pl.ds(2 * field, 2)].astype(F32)

    def coef_at(row):
        return [jnp.concatenate([coef[k, row]] * 2, axis=0) for k in range(5)]

    def first(row, carry):
        value = step_row(field_rows[row + 1], field_rows[row + 2], field_rows[row], coef_at(row))
        middle[row] = value.astype(BF16).astype(F32)
        return carry

    lax.fori_loop(0, 18, first, 0, unroll=3)
    middle[0] = jnp.where(flags_ref[0] == 1, 0.0, middle[0])
    middle[17] = jnp.where(flags_ref[1] == 1, 0.0, middle[17])

    def second(row, carry):
        value = step_row(middle[row + 1], middle[row + 2], middle[row], coef_at(row + 1))
        out_ref[row, 0] = value.astype(BF16)
        return carry

    lax.fori_loop(0, 16, second, 0, unroll=2)


def forecast(flags, state, s, z, m, low, high):
    whole = pl.BlockSpec((16, 512), lambda f: (0, 0))
    halo = pl.BlockSpec((17, 16, 512), lambda f: (0, 0, 0))
    return pl.pallas_call(
        forecast_kernel,
        grid=(8,),
        in_specs=[
            pl.BlockSpec(memory_space=pltpu.SMEM),
            pl.BlockSpec((16, 1, 16, 512), lambda f: (0, f, 0, 0)),
            whole,
            whole,
            whole,
            halo,
            halo,
        ],
        out_specs=pl.BlockSpec((16, 1, 16, 512), lambda f: (0, f, 0, 0)),
        out_shape=jax.ShapeDtypeStruct((16, 8, 16, 512), BF16),
        scratch_shapes=[
            pltpu.VMEM((256, 256), BF16),
            pltpu.VMEM((5, 18, 8, 512), F32),
            pltpu.VMEM((20, 16, 512), F32),
            pltpu.VMEM((18, 16, 512), F32),
        ],
        name="forecast",
    )(flags, state, s, z, m, low, high)


def left(parts):
    return jnp.concatenate(parts, axis=1)


def right(parts):
    high, low = parts
    top = jnp.concatenate([high, low], axis=1)
    bottom = jnp.concatenate([high, jnp.zeros_like(low)], axis=1)
    return jnp.concatenate([top, bottom], axis=0)


def product(a, b):
    both = dot(a, b)
    return both[:, :128] + both[:, 128:]


def weights_of(patches, members):
    spread = float(members - 1)
    rows = lax.broadcasted_iota(jnp.int32, (128, 128), 0)
    cols = lax.broadcasted_iota(jnp.int32, (128, 128), 1)
    eye = (rows == cols).astype(F32)
    work = []
    for observed, live, value, weight in patches:
        mean = jnp.sum(observed, axis=0, keepdims=True) * (1.0 / members)
        precision_w = weight * live
        root = jnp.sqrt(precision_w)
        scaled = (observed - mean) * root
        work.append({"a": scaled, "v": root * (value - mean)})
    for w in work:
        both = left(halves(w["a"]))
        gram = lax.dot_general(both, both, (((0,), (0,)), ((), ())), preferred_element_type=F32)
        w["g"] = gram[:128, :128] + gram[:128, 128:] + gram[128:, :128]
    for w in work:
        g = w["g"]
        square = jnp.sum(jnp.sum(g * g + (2.0 * spread) * (g * eye), axis=1, keepdims=True), axis=0, keepdims=True)
        scale = jnp.sqrt(square + spread * spread * members)
        inv = 1.0 / scale
        w["scale"], w["inv"] = scale, inv
        w["low"] = spread * inv
        w["y"] = g * inv + w["low"] * eye
        w["z0"] = jnp.ones((1, 1), F32)
    for sweep in range(ITERS):
        last = sweep == ITERS - 1
        for w in work:
            y = w["y"]
            y_parts = halves(y)
            y0 = w["low"] * w["z0"]
            w0 = w["z0"] * y0
            f0 = 1.5 - 0.5 * w0
            if sweep == 0:
                f = 1.5 * eye - 0.5 * y
                fq = -0.5 * eye
                w["next"] = (f, fq, f0, y_parts, None)
            else:
                zz = jnp.concatenate([left(w["z_parts"]), left(w["q_parts"])], axis=0)
                out = product(zz, right(y_parts))
                wq = out[128:] + w["z0"] * (w["low"] * w["q"] + w["z"])
                f = 1.5 * eye - 0.5 * out[:128]
                fq = -0.5 * wq
                w["next"] = (f, fq, f0, y_parts, zz)
        for w in work:
            f, fq, f0, y_parts, zz = w["next"]
            if sweep == 0:
                w["y"] = product(left(y_parts), right(halves(f)))
                w["z"], w["q"] = f, fq
            else:
                rhs = right(halves(f))
                lhs = zz if last else jnp.concatenate([zz, left(y_parts)], axis=0)
                out = product(lhs, rhs)
                w["z"] = out[:128]
                w["q"] = out[128:256] + w["z0"] * fq
                if not last:
                    w["y"] = out[256:]
            w["z0"] = w["z0"] * f0
            if not last:
                w["z_parts"], w["q_parts"] = halves(w["z"]), halves(w["q"])
    for w in work:
        z = right(halves(w["z"]))
        u = jnp.broadcast_to(w["v"], (8, 128))
        u = product(left(halves(u)), z)
        u = product(left(halves(u)), z)
        root = lax.rsqrt(w["scale"])
        w["u"] = u[:1] * root
        w["hat"] = w["a"] * root
        w["c1"] = math.sqrt(spread) * root
    big_rows = lax.broadcasted_iota(jnp.int32, (members, members), 0)
    big_cols = lax.broadcasted_iota(jnp.int32, (members, members), 1)
    big_eye = (big_rows == big_cols).astype(F32)
    result = []
    for w in work:
        hat_high, hat_low = halves(w["hat"])
        t = product(left((hat_high, hat_low)), right(halves(w["q"])))
        t = w["c1"] * t + w["u"]
        t_high, t_low = halves(t)
        nt = (((1,), (1,)), ((), ()))
        full = lax.dot_general(left((t_high, t_low)), left((hat_high, hat_high)), nt, preferred_element_type=F32)
        full = full + lax.dot_general(t_high, hat_low, nt, preferred_element_type=F32)
        result.append((full + (w["c1"] * w["z0"]) * big_eye).astype(BF16))
    return result


def selector(index_row):
    entry = lax.broadcasted_iota(jnp.int32, (1024, 128), 0)
    return (entry == index_row).astype(F32).astype(BF16)


def analysis_kernel(count_ref, x_ref, index_ref, value_ref, weight_ref, out_ref, held):
    slot = lax.broadcasted_iota(jnp.int32, (1, 128), 1)
    patches = []
    for p in range(4):
        for f in range(8):
            held[p, :, f * 128 : (f + 1) * 128] = x_ref[:, f, :, p * 128 : (p + 1) * 128].reshape(256, 128)
    for p in range(4):
        observed = dot(held[p], selector(index_ref[p : p + 1]))
        live = (slot < count_ref[0, p]).astype(F32)
        patches.append((observed, live, value_ref[p : p + 1], weight_ref[p : p + 1]))
    weights = weights_of(patches, 256)
    for p in range(4):
        for f in range(8):
            x = held[p, :, f * 128 : (f + 1) * 128].astype(F32)
            centre = jnp.sum(x, axis=0, keepdims=True) * (1.0 / 256)
            pert = (x - centre).astype(BF16)
            out = dot(weights[p], pert) + centre
            out_ref[:, f, :, p * 128 : (p + 1) * 128] = out.astype(BF16).reshape(16, 16, 128)


def analysis(count, x, index, value, weight):
    vmem = pl.BlockSpec(memory_space=pltpu.VMEM)
    return pl.pallas_call(
        analysis_kernel,
        in_specs=[pl.BlockSpec(memory_space=pltpu.SMEM), vmem, vmem, vmem, vmem],
        out_specs=vmem,
        out_shape=jax.ShapeDtypeStruct((16, 8, 16, 512), BF16),
        scratch_shapes=[pltpu.VMEM((4, 256, 1024), BF16)],
        compiler_params=pltpu.CompilerParams(vmem_limit_bytes=48 * 1024 * 1024),
        name="analysis",
    )(count, x, index, value, weight)


def result_kernel(x_ref, out_ref):
    flat = x_ref[:, 0].reshape(256, 512)
    out_ref[:, 0] = dot(row_picker(16, 0, 16, 16), flat).astype(BF16).reshape(16, 16, 512)


def result(x):
    spec = pl.BlockSpec((16, 1, 16, 512), lambda f: (0, f, 0, 0))
    return pl.pallas_call(
        result_kernel,
        grid=(8,),
        in_specs=[spec],
        out_specs=spec,
        out_shape=jax.ShapeDtypeStruct((16, 8, 16, 512), BF16),
        name="result",
    )(x)


def shards(state, s, z, m, obs_count, obs_index, obs_value, obs_weight):
    domains = lax.axis_size("domain")
    here = lax.axis_index("domain")
    south, north = edges(state, s, z, m)
    up = [(i, i + 1) for i in range(domains - 1)]
    down = [(i + 1, i) for i in range(domains - 1)]
    low = lax.ppermute(north, "domain", up)
    high = lax.ppermute(south, "domain", down)
    flags = jnp.stack([here == 0, here == domains - 1]).astype(jnp.int32)
    grown = forecast(flags, state, s, z, m, low, high)
    gathered = lax.all_to_all(grown, "member", split_axis=0, concat_axis=0, tiled=True)
    analysed = analysis(obs_count, gathered, obs_index[0], obs_value[0], obs_weight[0])
    back = lax.all_to_all(analysed, "member", split_axis=0, concat_axis=0, tiled=True)
    return result(back)


def solution(mesh):
    placed = (
        P("member", None, "domain", None),
        P("domain", None),
        P("domain", None),
        P("domain", None),
        P(("domain", "member"), None),
        P(("domain", "member"), None, None),
        P(("domain", "member"), None, None),
        P(("domain", "member"), None, None),
    )
    return jax.shard_map(
        shards,
        mesh=mesh,
        in_specs=placed,
        out_specs=P("member", None, "domain", None),
        check_vma=False,
    )
```

```python
import functools
import math

import jax
import jax.numpy as jnp
from jax import lax
from jax.experimental import pallas as pl
from jax.experimental.pallas import tpu as pltpu
from jax.sharding import PartitionSpec as P

ITERS = 6
F32 = jnp.float32
BF16 = jnp.bfloat16


def halves(x):
    high = x.astype(BF16)
    return high, (x - high.astype(F32)).astype(BF16)


def thirds(x):
    high = x.astype(BF16)
    rest = x - high.astype(F32)
    mid = rest.astype(BF16)
    return high, mid, (rest - mid.astype(F32)).astype(BF16)


def dot(a, b):
    return jnp.dot(a, b, preferred_element_type=F32)


ORDER = (3, 5, 2, 6, 4, 1, 7, 0)
BACK = tuple(ORDER.index((8 - d) % 8) for d in ORDER)
PIECE = (2, 8, 16, 256)
FIELDS = 4


def row_picker(rows, first_row):
    out = lax.broadcasted_iota(jnp.int32, (rows * 16, 256), 0)
    src = lax.broadcasted_iota(jnp.int32, (rows * 16, 256), 1)
    row = (out >> 4) + first_row
    hit = jnp.logical_and((src & 15) == row, (src >> 4) == (out & 15))
    return hit.astype(F32).astype(BF16)


def place():
    member = lax.axis_index("member")
    return member >> 1, member & 1


def coefficients(s, z, m):
    return (1.0 - 4.0 * s, s - 0.5 * z, s + 0.5 * z, s - 0.5 * m, s + 0.5 * m)


def step_row(centre, north, south, coef):
    east = pltpu.roll(centre, 511, 1)
    west = pltpu.roll(centre, 1, 1)
    c, e, w, n, so = coef
    return centre * c + east * e + west * w + north * n + south * so


def forecast_rows(edge, own_ref, sib_ref, numbers, halo_ref, outs, pick, coef, fields, middle, ready):
    step = pl.program_id(0)
    z, c = place()
    base = 12 * c - 2 if edge else 2 + 4 * c

    @pl.when(step == 0)
    def _():
        pick[...] = row_picker(8, base)
        for j in range(6):
            row = jnp.clip(base + 1 + j, 0, 15)
            for k, value in enumerate(coefficients(*[ref[pl.ds(row, 1)] for ref in numbers])):
                coef[k, j] = jnp.broadcast_to(value, (8, 512))
        if edge:
            part = halo_ref[8, 0].astype(F32)
            rows = [part[3 * k : 3 * k + 1] + part[3 * k + 1 : 3 * k + 2] + part[3 * k + 2 : 3 * k + 3] for k in range(3)]
            for k, value in enumerate(coefficients(*rows)):
                coef[k, 5 * c] = jnp.broadcast_to(value, (8, 512))

    if edge:
        domain = lax.axis_index("domain")
        outside = jnp.where(c == 0, domain == 0, domain == lax.axis_size("domain") - 1)

    def coef_at(j):
        return [jnp.concatenate([coef[k, j]] * 4, axis=0) for k in range(5)]

    def one_field(f, carry):
        fields[:, :16] = dot(pick[...], own_ref[:, f].reshape(256, 512)).reshape(8, 16, 512)
        fields[:, 16:] = dot(pick[...], sib_ref[:, f].reshape(256, 512)).reshape(8, 16, 512)
        if edge:
            fields[pl.ds(6 * c, 2)] = halo_ref[FIELDS * step + f].astype(F32)
        for j in range(6):
            value = step_row(fields[j + 1], fields[j + 2], fields[j], coef_at(j))
            middle[j] = value.astype(BF16).astype(F32)
        if edge:

            @pl.when(outside)
            def _():
                middle[5 * c] = jnp.zeros((32, 512), F32)

        for j in range(4):
            value = step_row(middle[j + 1], middle[j + 2], middle[j], coef_at(j + 1)).astype(BF16)
            ready[2 * j] = value[:, :256]
            ready[2 * j + 1] = value[:, 256:]
        for k, out_ref in enumerate(outs):
            out_ref[:, f] = ready[(z + ORDER[k]) & 7].reshape(2, 16, 256)
        return carry

    lax.fori_loop(0, FIELDS, one_field, 0)


def inner_kernel(own_ref, sib_ref, s_ref, z_ref, m_ref, *rest):
    outs, halo_ref, scratch = rest[:8], rest[8], rest[9:]
    step = pl.program_id(0)
    numbers = (s_ref, z_ref, m_ref)
    forecast_rows(False, own_ref, sib_ref, numbers, None, outs, *scratch[:5])
    pick = scratch[5]
    _, c = place()

    @pl.when(step == 0)
    def _():
        pick[...] = row_picker(2, 14 * c)
        parts = []
        for ref in numbers:
            parts += list(thirds(ref[pl.ds(15 * c, 1)]))
        parts.append(jnp.zeros((23, 512), BF16))
        halo_ref[8, 0] = jnp.concatenate(parts, axis=0)
        halo_ref[8, 1] = jnp.zeros((32, 512), BF16)

    def one_field(f, carry):
        own = dot(pick[...], own_ref[:, f].reshape(256, 512)).astype(BF16)
        sib = dot(pick[...], sib_ref[:, f].reshape(256, 512)).astype(BF16)
        halo_ref[FIELDS * step + f, :, :16] = sib.reshape(2, 16, 512)
        halo_ref[FIELDS * step + f, :, 16:] = own.reshape(2, 16, 512)
        return carry

    lax.fori_loop(0, FIELDS, one_field, 0)


def edge_kernel(own_ref, sib_ref, s_ref, z_ref, m_ref, halo_ref, *rest):
    forecast_rows(True, own_ref, sib_ref, (s_ref, z_ref, m_ref), halo_ref, rest[:8], *rest[8:])


FORECAST_SCRATCH = (
    ((128, 256), BF16),
    ((5, 6, 8, 512), F32),
    ((8, 32, 512), F32),
    ((6, 32, 512), F32),
    ((8, 32, 256), BF16),
)


def forecast(own, sib, numbers, halo=None):
    block = pl.BlockSpec((16, FIELDS, 16, 512), lambda f: (0, f, 0, 0))
    whole = pl.BlockSpec((16, 512), lambda f: (0, 0))
    halo_spec = pl.BlockSpec((9, 2, 32, 512), lambda f: (0, 0, 0, 0))
    piece = pl.BlockSpec((2, FIELDS, 16, 256), lambda f: (0, f, 0, 0))
    pieces = [jax.ShapeDtypeStruct(PIECE, BF16)] * 8
    scratch = [pltpu.VMEM(*s) for s in FORECAST_SCRATCH]
    cost = pl.CostEstimate(flops=300_000_000, bytes_accessed=6_000_000, transcendentals=0)
    if halo is None:
        return pl.pallas_call(
            inner_kernel,
            grid=(8 // FIELDS,),
            in_specs=[block, block, whole, whole, whole],
            out_specs=[piece] * 8 + [halo_spec],
            out_shape=pieces + [jax.ShapeDtypeStruct((9, 2, 32, 512), BF16)],
            scratch_shapes=scratch + [pltpu.VMEM((32, 256), BF16)],
            cost_estimate=cost,
            name="inner_forecast",
        )(own, sib, *numbers)
    return pl.pallas_call(
        edge_kernel,
        grid=(8 // FIELDS,),
        in_specs=[block, block, whole, whole, whole, halo_spec],
        out_specs=[piece] * 8,
        out_shape=pieces,
        scratch_shapes=scratch,
        cost_estimate=cost,
        name="edge_forecast",
    )(own, sib, *numbers, halo)


def left(parts):
    return jnp.concatenate(parts, axis=1)


def right(parts):
    high, low = parts
    top = jnp.concatenate([high, low], axis=1)
    bottom = jnp.concatenate([high, jnp.zeros_like(low)], axis=1)
    return jnp.concatenate([top, bottom], axis=0)


def product(a, b):
    both = dot(a, b)
    return both[:, :128] + both[:, 128:]


def weights_of(patches, members):
    spread = float(members - 1)
    rows = lax.broadcasted_iota(jnp.int32, (128, 128), 0)
    cols = lax.broadcasted_iota(jnp.int32, (128, 128), 1)
    eye = (rows == cols).astype(F32)
    work = []
    for observed, live, value, weight in patches:
        mean = jnp.sum(observed, axis=0, keepdims=True) * (1.0 / members)
        precision_w = weight * live
        root = jnp.sqrt(precision_w)
        scaled = (observed - mean) * root
        work.append({"a": scaled, "v": root * (value - mean)})
    for w in work:
        both = left(halves(w["a"]))
        gram = lax.dot_general(both, both, (((0,), (0,)), ((), ())), preferred_element_type=F32)
        w["g"] = gram[:128, :128] + gram[:128, 128:] + gram[128:, :128]
    for w in work:
        g = w["g"]
        square = jnp.sum(jnp.sum(g * g + (2.0 * spread) * (g * eye), axis=1, keepdims=True), axis=0, keepdims=True)
        scale = jnp.sqrt(square + spread * spread * members)
        inv = 1.0 / scale
        w["scale"], w["inv"] = scale, inv
        w["low"] = spread * inv
        w["y"] = g * inv + w["low"] * eye
        w["z0"] = jnp.ones((1, 1), F32)
    for sweep in range(ITERS):
        last = sweep == ITERS - 1
        for w in work:
            y = w["y"]
            y_parts = halves(y)
            y0 = w["low"] * w["z0"]
            w0 = w["z0"] * y0
            f0 = 1.5 - 0.5 * w0
            if sweep == 0:
                f = 1.5 * eye - 0.5 * y
                fq = -0.5 * eye
                w["next"] = (f, fq, f0, y_parts, None)
            else:
                zz = jnp.concatenate([left(w["z_parts"]), left(w["q_parts"])], axis=0)
                out = product(zz, right(y_parts))
                wq = out[128:] + w["z0"] * (w["low"] * w["q"] + w["z"])
                f = 1.5 * eye - 0.5 * out[:128]
                fq = -0.5 * wq
                w["next"] = (f, fq, f0, y_parts, zz)
        for w in work:
            f, fq, f0, y_parts, zz = w["next"]
            if sweep == 0:
                w["y"] = product(left(y_parts), right(halves(f)))
                w["z"], w["q"] = f, fq
            else:
                rhs = right(halves(f))
                lhs = zz if last else jnp.concatenate([zz, left(y_parts)], axis=0)
                out = product(lhs, rhs)
                w["z"] = out[:128]
                w["q"] = out[128:256] + w["z0"] * fq
                if not last:
                    w["y"] = out[256:]
            w["z0"] = w["z0"] * f0
            if not last:
                w["z_parts"], w["q_parts"] = halves(w["z"]), halves(w["q"])
    for w in work:
        z = right(halves(w["z"]))
        u = jnp.broadcast_to(w["v"], (8, 128))
        u = product(left(halves(u)), z)
        u = product(left(halves(u)), z)
        root = lax.rsqrt(w["scale"])
        w["u"] = u[:1] * root
        w["hat"] = w["a"] * root
        w["c1"] = math.sqrt(spread) * root
    big_rows = lax.broadcasted_iota(jnp.int32, (members, members), 0)
    big_cols = lax.broadcasted_iota(jnp.int32, (members, members), 1)
    big_eye = (big_rows == big_cols).astype(F32)
    result = []
    for w in work:
        hat_high, hat_low = halves(w["hat"])
        t = product(left((hat_high, hat_low)), right(halves(w["q"])))
        t = w["c1"] * t + w["u"]
        t_high, t_low = halves(t)
        nt = (((1,), (1,)), ((), ()))
        full = lax.dot_general(left((t_high, t_low)), left((hat_high, hat_high)), nt, preferred_element_type=F32)
        full = full + lax.dot_general(t_high, hat_low, nt, preferred_element_type=F32)
        result.append((full + (w["c1"] * w["z0"]) * big_eye).astype(BF16))
    return result


def selector(index_row):
    entry = lax.broadcasted_iota(jnp.int32, (1024, 128), 0)
    return (entry == index_row).astype(F32).astype(BF16)


def analysis_kernel(edge, even_ref, odd_ref, *rest):
    pieces, outs, held = rest[:8], rest[8:16], rest[16]
    z, _ = place()
    slot = lax.broadcasted_iota(jnp.int32, (1, 128), 1).astype(F32)
    for k in range(8):
        for g in range(2):
            at = k * 32 + g * 16
            for f in range(8):
                for p in range(2):
                    held[p, at : at + 16, f * 128 : (f + 1) * 128] = pieces[k][g, f, :, p * 128 : (p + 1) * 128]
    patches = []
    for p in range(2):
        patch = pl.ds(2 * (z & 1) + p, 1)
        obs = jnp.where((z & 1) == int(edge), even_ref[0, patch], odd_ref[0, patch])
        index = obs[:, :128].astype(jnp.int32)
        observed = dot(held[p], selector(index))
        live = (slot < obs[:, 384:]).astype(F32)
        patches.append((observed, live, obs[:, 128:256], obs[:, 256:384]))
    weights = weights_of(patches, 256)
    for p in range(2):
        for f in range(8):
            x = held[p, :, f * 128 : (f + 1) * 128].astype(F32)
            centre = jnp.sum(x, axis=0, keepdims=True) * (1.0 / 256)
            pert = (x - centre).astype(BF16)
            out = (dot(weights[p], pert) + centre).astype(BF16)
            for k in range(8):
                at = BACK[k] * 32
                outs[k][:, f, :, p * 128 : (p + 1) * 128] = out[at : at + 32].reshape(2, 16, 128)


def analysis(edge, obs, pieces):
    vmem = pl.BlockSpec(memory_space=pltpu.VMEM)
    return pl.pallas_call(
        functools.partial(analysis_kernel, edge),
        in_specs=[vmem] * 10,
        out_specs=[vmem] * 8,
        out_shape=[jax.ShapeDtypeStruct(PIECE, BF16)] * 8,
        scratch_shapes=[pltpu.VMEM((2, 256, 1024), BF16)],
        compiler_params=pltpu.CompilerParams(vmem_limit_bytes=40 * 1024 * 1024),
        cost_estimate=pl.CostEstimate(flops=2_000_000_000, bytes_accessed=6_000_000, transcendentals=0),
        name="edge_analysis" if edge else "inner_analysis",
    )(*obs, *pieces)


def pack_kernel(*refs):
    z, _ = place()
    for k in range(8):
        refs[8][(z - ORDER[k]) & 7] = refs[k][0]


def pack(pieces, name):
    return pl.pallas_call(
        pack_kernel,
        grid=(1,),
        in_specs=[pl.BlockSpec((1, 8, 16, 256), lambda i: (1, 0, 0, 0))] * 8,
        out_specs=pl.BlockSpec((8, 8, 16, 256), lambda i: (0, 0, 0, 0)),
        out_shape=jax.ShapeDtypeStruct((8, 8, 16, 256), BF16),
        name=name,
    )(*pieces)


def result_kernel(*refs):
    mine, theirs, out_ref, pick, rows = refs[:16], refs[16:18], refs[18], refs[19], refs[20]
    z, c = place()

    @pl.when(pl.program_id(0) == 0)
    def _():
        pick[...] = row_picker(16, 0)

    def one_field(f, carry):
        for chunk in range(2):
            own_base = 12 * c if chunk else 4 + 4 * c
            sib_base = 12 - 12 * c if chunk else 8 - 4 * c
            for k in range(8):
                rows[2 * own_base + ((z - ORDER[k]) & 7)] = mine[8 * chunk + k][0, f]
            for source in range(8):
                rows[2 * sib_base + source] = theirs[chunk][source, f]
        both = rows[...].reshape(16, 2, 16, 256)
        for h in range(2):
            out = dot(pick[...], both[:, h].reshape(256, 256)).astype(BF16)
            out_ref[:, f, :, h * 256 : (h + 1) * 256] = out.reshape(16, 16, 256)
        return carry

    lax.fori_loop(0, FIELDS, one_field, 0)


def result(mine, theirs):
    own = pl.BlockSpec((1, FIELDS, 16, 256), lambda f: (0, f, 0, 0))
    sib = pl.BlockSpec((8, FIELDS, 16, 256), lambda f: (0, f, 0, 0))
    return pl.pallas_call(
        result_kernel,
        grid=(8 // FIELDS,),
        in_specs=[own] * 16 + [sib] * 2,
        out_specs=pl.BlockSpec((16, FIELDS, 16, 512), lambda f: (0, f, 0, 0)),
        out_shape=jax.ShapeDtypeStruct((16, 8, 16, 512), BF16),
        scratch_shapes=[pltpu.VMEM((256, 256), BF16), pltpu.VMEM((32, 16, 256), BF16)],
        name="result",
    )(*mine, *theirs)


def obs_pairs():
    def target(row, odd):
        return 2 * (2 * (row % 4) + odd) + row // 8

    inner = range(4, 12)
    first = [(row, target(row, int(row not in inner))) for row in range(16)]
    return first, [(row, target(row, int(row in inner))) for row in range(16)]


def swap(x):
    return lax.ppermute(x, "member", [(i, i ^ 1) for i in range(16)])


def around(x, distance):
    return lax.ppermute(x, "member", [(i, (i + 2 * distance) % 16) for i in range(16)])


def exchange(pieces):
    return [around(x, d) if d else x for x, d in zip(pieces, ORDER)]


def shards(state, s, z, m, obs_count, obs_index, obs_value, obs_weight):
    numbers = (s, z, m)
    count = jnp.broadcast_to(obs_count[:, :, None], obs_index.shape)
    obs = jnp.concatenate([obs_index.astype(F32), obs_value, obs_weight, count.astype(F32)], axis=2)
    sib = swap(state)
    obs = [lax.ppermute(obs, "member", pairs) for pairs in obs_pairs()]
    *inner, halo = forecast(state, sib, numbers)
    domains = lax.axis_size("domain")
    pairs = []
    for chip in range(8):
        for d in range(domains - 1):
            pairs.append(((2 * chip + 1) * domains + d, 2 * chip * domains + d + 1))
            pairs.append((2 * chip * domains + d + 1, (2 * chip + 1) * domains + d))
    inner = exchange(inner)
    halo = lax.ppermute(halo, ("member", "domain"), pairs)
    outer = exchange(forecast(state, sib, numbers, halo))
    inner = exchange(analysis(False, obs, inner))
    inner_sib = swap(pack(inner, "inner_pack"))
    outer = exchange(analysis(True, obs, outer))
    outer_sib = swap(pack(outer, "edge_pack"))
    return result(inner + outer, [inner_sib, outer_sib])


def solution(mesh):
    placed = (
        P("member", None, "domain", None),
        P("domain", None),
        P("domain", None),
        P("domain", None),
        P(("domain", "member"), None),
        P(("domain", "member"), None, None),
        P(("domain", "member"), None, None),
        P(("domain", "member"), None, None),
    )
    return jax.shard_map(
        shards,
        mesh=mesh,
        in_specs=placed,
        out_specs=P("member", None, "domain", None),
        check_vma=False,
    )
```

```python
import functools
import math

import jax
import jax.numpy as jnp
from jax import lax
from jax.experimental import pallas as pl
from jax.experimental.pallas import tpu as pltpu
from jax.sharding import PartitionSpec as P

ITERS = 6
F32 = jnp.float32
BF16 = jnp.bfloat16


def halves(x):
    high = x.astype(BF16)
    return high, (x - high.astype(F32)).astype(BF16)


def thirds(x):
    high = x.astype(BF16)
    rest = x - high.astype(F32)
    mid = rest.astype(BF16)
    return high, mid, (rest - mid.astype(F32)).astype(BF16)


def dot(a, b):
    return jnp.dot(a, b, preferred_element_type=F32)


ORDER = (3, 5, 2, 6, 4, 1, 7, 0)
BACK = tuple(ORDER.index((8 - d) % 8) for d in ORDER)
PIECE = (2, 8, 16, 256)


def row_picker(rows, first_row):
    out = lax.broadcasted_iota(jnp.int32, (rows * 16, 256), 0)
    src = lax.broadcasted_iota(jnp.int32, (rows * 16, 256), 1)
    row = (out >> 4) + first_row
    hit = jnp.logical_and((src & 15) == row, (src >> 4) == (out & 15))
    return hit.astype(F32).astype(BF16)


def place():
    member = lax.axis_index("member")
    return member >> 1, member & 1


def coefficients(s, z, m):
    return (1.0 - 4.0 * s, s - 0.5 * z, s + 0.5 * z, s - 0.5 * m, s + 0.5 * m)


def step_row(centre, north, south, coef):
    east = pltpu.roll(centre, 511, 1)
    west = pltpu.roll(centre, 1, 1)
    c, e, w, n, so = coef
    return centre * c + east * e + west * w + north * n + south * so


def two_steps(rows_at, coef_at, outside, groups, middle, ready):
    coefs = [coef_at(j) for j in range(6)]
    rows = [rows_at(j) for j in range(8)]
    for j in range(6):
        value = step_row(rows[j + 1], rows[j + 2], rows[j], coefs[j])
        middle[j] = value.astype(BF16).astype(F32)
    if outside is not None:
        beyond, at = outside

        @pl.when(beyond)
        def _():
            middle[at] = jnp.zeros((16 * groups, 512), F32)

    for j in range(4):
        value = step_row(middle[j + 1], middle[j + 2], middle[j], coefs[j + 1]).astype(BF16)
        ready[2 * j] = value[:, :256]
        ready[2 * j + 1] = value[:, 256:]


def put_coef(coef, j, numbers):
    for k, value in enumerate(coefficients(*numbers)):
        coef[k, j] = jnp.broadcast_to(value, (8, 512))


def inner_field(pick, flat, c, coef, fields, middle, ready):
    picked = dot(pick[...], flat)
    fields[...] = picked[:128].reshape(8, 16, 512)
    two_steps(
        lambda j: fields[j],
        lambda j: [jnp.concatenate([coef[k, j]] * 2, axis=0) for k in range(5)],
        None,
        1,
        middle,
        ready,
    )
    return picked[128:].astype(BF16).reshape(2, 16, 512)


def own_kernel(own_ref, numbers, inner_coef, edge_coef, part_ref, halo_ref, pick, fields, middle, ready):
    z, c = place()
    pick[:128] = row_picker(8, 2 + 4 * c)
    pick[128:] = row_picker(2, 14 * c)

    def number_rows(row):
        return [numbers[i, pl.ds(row, 1)] for i in range(3)]

    for j in range(6):
        put_coef(inner_coef, j, number_rows(3 + 4 * c + j))
        put_coef(edge_coef, j, number_rows(jnp.clip(12 * c - 1 + j, 0, 15)))
    parts = []
    for value in number_rows(15 * c):
        parts += list(thirds(value))
    parts.append(jnp.zeros((7, 512), BF16))
    halo_ref[8, 0] = jnp.concatenate(parts, axis=0)
    halo_ref[8, 1] = jnp.zeros((16, 512), BF16)

    def one_field(f, carry):
        flat = own_ref[:, f].reshape(256, 512)
        halo_ref[f] = inner_field(pick, flat, c, inner_coef, fields, middle, ready)
        for k in range(8):
            part_ref[k, f] = ready[(z + ORDER[k]) & 7]
        return carry

    lax.fori_loop(0, 8, one_field, 0)


def sib_kernel(sib_ref, coef, part_ref, own_halo_ref, *rest):
    outs, halo_ref = rest[:8], rest[8]
    pick, fields, middle, ready = rest[9:]
    z, c = place()
    pick[:128] = row_picker(8, 2 + 4 * c)
    pick[128:] = row_picker(2, 14 * c)

    def one_field(f, carry):
        flat = sib_ref[:, f].reshape(256, 512)
        halo_ref[f, :, :16] = inner_field(pick, flat, c, coef, fields, middle, ready)
        halo_ref[f, :, 16:] = own_halo_ref[f]
        for k, out_ref in enumerate(outs):
            out_ref[0, f] = part_ref[k, f]
            out_ref[1, f] = ready[(z + ORDER[k]) & 7]
        return carry

    lax.fori_loop(0, 8, one_field, 0)
    halo_ref[8, :, :16] = own_halo_ref[8]
    halo_ref[8, :, 16:] = jnp.zeros((2, 16, 512), BF16)


def edge_kernel(own_ref, sib_ref, coef_ref, halo_ref, *rest):
    outs = rest[:8]
    pick, coef, fields, middle, ready = rest[8:]
    z, c = place()
    pick[...] = row_picker(8, 12 * c - 2)
    coef[...] = coef_ref[...]
    part = halo_ref[8, 0].astype(F32)
    put_coef(coef, 5 * c, [part[3 * k : 3 * k + 1] + part[3 * k + 1 : 3 * k + 2] + part[3 * k + 2 : 3 * k + 3] for k in range(3)])
    domain = lax.axis_index("domain")
    outside = jnp.where(c == 0, domain == 0, domain == lax.axis_size("domain") - 1)

    def one_field(f, carry):
        fields[:, :16] = dot(pick[...], own_ref[:, f].reshape(256, 512)).reshape(8, 16, 512)
        fields[:, 16:] = dot(pick[...], sib_ref[:, f].reshape(256, 512)).reshape(8, 16, 512)
        fields[pl.ds(6 * c, 2)] = halo_ref[f].astype(F32)
        two_steps(
            lambda j: fields[j],
            lambda j: [jnp.concatenate([coef[k, j]] * 4, axis=0) for k in range(5)],
            (outside, 5 * c),
            2,
            middle,
            ready,
        )
        for k, out_ref in enumerate(outs):
            out_ref[:, f] = ready[(z + ORDER[k]) & 7].reshape(2, 16, 256)
        return carry

    lax.fori_loop(0, 8, one_field, 0)


VMEM = pl.BlockSpec(memory_space=pltpu.VMEM)
ANY = pl.BlockSpec(memory_space=pl.ANY)
LIMIT = pltpu.CompilerParams(vmem_limit_bytes=40 * 1024 * 1024)


def cost(flops, transfer):
    return pl.CostEstimate(flops=flops, bytes_accessed=transfer, transcendentals=0)


def own_forecast(own, numbers):
    shapes = [((5, 6, 8, 512), F32)] * 2 + [((8, 8, 16, 256), BF16), ((9, 2, 16, 512), BF16)]
    return pl.pallas_call(
        own_kernel,
        in_specs=[VMEM] * 2,
        out_specs=[VMEM] * 4,
        out_shape=[jax.ShapeDtypeStruct(*shape) for shape in shapes],
        scratch_shapes=[
            pltpu.VMEM((160, 256), BF16),
            pltpu.VMEM((8, 16, 512), F32),
            pltpu.VMEM((6, 16, 512), F32),
            pltpu.VMEM((8, 16, 256), BF16),
        ],
        compiler_params=LIMIT,
        cost_estimate=cost(300_000_000, 6_000_000),
        name="own_forecast",
    )(own, numbers)


def sib_forecast(sib, coef, part, halo):
    return pl.pallas_call(
        sib_kernel,
        in_specs=[VMEM] * 4,
        out_specs=[VMEM] * 9,
        out_shape=[jax.ShapeDtypeStruct(PIECE, BF16)] * 8 + [jax.ShapeDtypeStruct((9, 2, 32, 512), BF16)],
        scratch_shapes=[
            pltpu.VMEM((160, 256), BF16),
            pltpu.VMEM((8, 16, 512), F32),
            pltpu.VMEM((6, 16, 512), F32),
            pltpu.VMEM((8, 16, 256), BF16),
        ],
        compiler_params=LIMIT,
        cost_estimate=cost(300_000_000, 6_000_000),
        name="sib_forecast",
    )(sib, coef, part, halo)


def edge_forecast(own, sib, coef, halo):
    return pl.pallas_call(
        edge_kernel,
        in_specs=[VMEM] * 4,
        out_specs=[VMEM] * 8,
        out_shape=[jax.ShapeDtypeStruct(PIECE, BF16)] * 8,
        scratch_shapes=[
            pltpu.VMEM((128, 256), BF16),
            pltpu.VMEM((5, 6, 8, 512), F32),
            pltpu.VMEM((8, 32, 512), F32),
            pltpu.VMEM((6, 32, 512), F32),
            pltpu.VMEM((8, 32, 256), BF16),
        ],
        compiler_params=LIMIT,
        cost_estimate=cost(300_000_000, 6_000_000),
        name="edge_forecast",
    )(own, sib, coef, halo)


def left(parts):
    return jnp.concatenate(parts, axis=1)


def right(parts):
    high, low = parts
    top = jnp.concatenate([high, low], axis=1)
    bottom = jnp.concatenate([high, jnp.zeros_like(low)], axis=1)
    return jnp.concatenate([top, bottom], axis=0)


def product(a, b):
    both = dot(a, b)
    return both[:, :128] + both[:, 128:]


def weights_of(patches, members):
    spread = float(members - 1)
    rows = lax.broadcasted_iota(jnp.int32, (128, 128), 0)
    cols = lax.broadcasted_iota(jnp.int32, (128, 128), 1)
    eye = (rows == cols).astype(F32)
    work = []
    for observed, live, value, weight in patches:
        mean = jnp.sum(observed, axis=0, keepdims=True) * (1.0 / members)
        precision_w = weight * live
        root = jnp.sqrt(precision_w)
        scaled = (observed - mean) * root
        work.append({"a": scaled, "v": root * (value - mean)})
    for w in work:
        both = left(halves(w["a"]))
        gram = lax.dot_general(both, both, (((0,), (0,)), ((), ())), preferred_element_type=F32)
        w["g"] = gram[:128, :128] + gram[:128, 128:] + gram[128:, :128]
    for w in work:
        g = w["g"]
        square = jnp.sum(jnp.sum(g * g + (2.0 * spread) * (g * eye), axis=1, keepdims=True), axis=0, keepdims=True)
        scale = jnp.sqrt(square + spread * spread * members)
        inv = 1.0 / scale
        w["scale"], w["inv"] = scale, inv
        w["low"] = spread * inv
        w["y"] = g * inv + w["low"] * eye
        w["z0"] = jnp.ones((1, 1), F32)
    for sweep in range(ITERS):
        last = sweep == ITERS - 1
        for w in work:
            y = w["y"]
            y_parts = halves(y)
            y0 = w["low"] * w["z0"]
            w0 = w["z0"] * y0
            f0 = 1.5 - 0.5 * w0
            if sweep == 0:
                f = 1.5 * eye - 0.5 * y
                fq = -0.5 * eye
                w["next"] = (f, fq, f0, y_parts, None)
            else:
                zz = jnp.concatenate([left(w["z_parts"]), left(w["q_parts"])], axis=0)
                out = product(zz, right(y_parts))
                wq = out[128:] + w["z0"] * (w["low"] * w["q"] + w["z"])
                f = 1.5 * eye - 0.5 * out[:128]
                fq = -0.5 * wq
                w["next"] = (f, fq, f0, y_parts, zz)
        for w in work:
            f, fq, f0, y_parts, zz = w["next"]
            if sweep == 0:
                w["y"] = product(left(y_parts), right(halves(f)))
                w["z"], w["q"] = f, fq
            else:
                rhs = right(halves(f))
                lhs = zz if last else jnp.concatenate([zz, left(y_parts)], axis=0)
                out = product(lhs, rhs)
                w["z"] = out[:128]
                w["q"] = out[128:256] + w["z0"] * fq
                if not last:
                    w["y"] = out[256:]
            w["z0"] = w["z0"] * f0
            if not last:
                w["z_parts"], w["q_parts"] = halves(w["z"]), halves(w["q"])
    for w in work:
        z = right(halves(w["z"]))
        u = jnp.broadcast_to(w["v"], (8, 128))
        u = product(left(halves(u)), z)
        u = product(left(halves(u)), z)
        root = lax.rsqrt(w["scale"])
        w["u"] = u[:1] * root
        w["hat"] = w["a"] * root
        w["c1"] = math.sqrt(spread) * root
    big_rows = lax.broadcasted_iota(jnp.int32, (members, members), 0)
    big_cols = lax.broadcasted_iota(jnp.int32, (members, members), 1)
    big_eye = (big_rows == big_cols).astype(F32)
    result = []
    for w in work:
        hat_high, hat_low = halves(w["hat"])
        t = product(left((hat_high, hat_low)), right(halves(w["q"])))
        t = w["c1"] * t + w["u"]
        t_high, t_low = halves(t)
        nt = (((1,), (1,)), ((), ()))
        full = lax.dot_general(left((t_high, t_low)), left((hat_high, hat_high)), nt, preferred_element_type=F32)
        full = full + lax.dot_general(t_high, hat_low, nt, preferred_element_type=F32)
        result.append((full + (w["c1"] * w["z0"]) * big_eye).astype(BF16))
    return result


def selector(index_row):
    entry = lax.broadcasted_iota(jnp.int32, (1024, 128), 0)
    return (entry == index_row).astype(F32).astype(BF16)


def analysis_kernel(edge, even_ref, odd_ref, *rest):
    pieces, outs, held = rest[:8], rest[8:16], rest[16]
    z, _ = place()
    slot = lax.broadcasted_iota(jnp.int32, (1, 128), 1).astype(F32)
    for k in range(8):
        for g in range(2):
            at = k * 32 + g * 16
            for f in range(8):
                for p in range(2):
                    held[p, at : at + 16, f * 128 : (f + 1) * 128] = pieces[k][g, f, :, p * 128 : (p + 1) * 128]
    patches = []
    for p in range(2):
        patch = pl.ds(2 * (z & 1) + p, 1)
        index, value, weight, count = [
            jnp.where((z & 1) == int(edge), even_ref[0, i, patch], odd_ref[0, i, patch]) for i in range(4)
        ]
        observed = dot(held[p], selector(index.astype(jnp.int32)))
        patches.append((observed, (slot < count).astype(F32), value, weight))
    weights = weights_of(patches, 256)
    for p in range(2):
        for f in range(8):
            x = held[p, :, f * 128 : (f + 1) * 128].astype(F32)
            centre = jnp.sum(x, axis=0, keepdims=True) * (1.0 / 256)
            pert = (x - centre).astype(BF16)
            out = (dot(weights[p], pert) + centre).astype(BF16)
            for k in range(8):
                at = BACK[k] * 32
                outs[k][:, f, :, p * 128 : (p + 1) * 128] = out[at : at + 32].reshape(2, 16, 128)


def analysis(edge, obs, pieces):
    return pl.pallas_call(
        functools.partial(analysis_kernel, edge),
        in_specs=[VMEM] * 10,
        out_specs=[VMEM] * 8,
        out_shape=[jax.ShapeDtypeStruct(PIECE, BF16)] * 8,
        scratch_shapes=[pltpu.VMEM((2, 256, 1024), BF16)],
        compiler_params=LIMIT,
        cost_estimate=cost(2_000_000_000, 6_000_000),
        name="edge_analysis" if edge else "inner_analysis",
    )(*obs, *pieces)


def pack_kernel(*refs):
    z, _ = place()
    for k in range(8):
        refs[8][(z - ORDER[k]) & 7] = refs[k][1]


def pack(pieces, name):
    return pl.pallas_call(
        pack_kernel,
        in_specs=[VMEM] * 8,
        out_specs=VMEM,
        compiler_params=LIMIT,
        out_shape=jax.ShapeDtypeStruct((8, 8, 16, 256), BF16),
        name=name,
    )(*pieces)


def result_kernel(*refs):
    mine, theirs, out_ref, pick, rows, ready, sent = refs[:16], refs[16:18], refs[18], refs[19], refs[20], refs[21], refs[22]
    z, c = place()
    pick[...] = row_picker(16, 0)

    def send(f):
        return pltpu.make_async_copy(ready.at[f], out_ref.at[:, f], sent.at[f])

    def one_field(f, carry):
        for chunk in range(2):
            own_base = 12 * c if chunk else 4 + 4 * c
            sib_base = 12 - 12 * c if chunk else 8 - 4 * c
            for k in range(8):
                rows[2 * own_base + ((z - ORDER[k]) & 7)] = mine[8 * chunk + k][0, f]
            for source in range(8):
                rows[2 * sib_base + source] = theirs[chunk][source, f]
        both = rows[...].reshape(16, 2, 16, 256)
        for h in range(2):
            out = dot(pick[...], both[:, h].reshape(256, 256)).astype(BF16)
            ready[f, :, :, h * 256 : (h + 1) * 256] = out.reshape(16, 16, 256)
        send(f).start()
        return carry

    def finish(f, carry):
        send(f).wait()
        return carry

    lax.fori_loop(0, 8, one_field, 0)
    lax.fori_loop(0, 8, finish, 0)


def result(mine, theirs):
    return pl.pallas_call(
        result_kernel,
        in_specs=[VMEM] * 18,
        out_specs=pl.BlockSpec(memory_space=pl.ANY),
        out_shape=jax.ShapeDtypeStruct((16, 8, 16, 512), BF16),
        scratch_shapes=[
            pltpu.VMEM((256, 256), BF16),
            pltpu.VMEM((32, 16, 256), BF16),
            pltpu.VMEM((8, 16, 16, 512), BF16),
            pltpu.SemaphoreType.DMA((8,)),
        ],
        compiler_params=LIMIT,
        name="result",
    )(*mine, *theirs)


def obs_pairs():
    def target(row, odd):
        return 2 * (2 * (row % 4) + odd) + row // 8

    inner = range(4, 12)
    first = [(row, target(row, int(row not in inner))) for row in range(16)]
    return first, [(row, target(row, int(row in inner))) for row in range(16)]


def swap(x):
    return lax.ppermute(x, "member", [(i, i ^ 1) for i in range(16)])


def around(x, distance):
    return lax.ppermute(x, "member", [(i, (i + 2 * distance) % 16) for i in range(16)])


def exchange(pieces):
    return [around(x, d) if d else x for x, d in zip(pieces, ORDER)]


def shards(state, s, z, m, obs_count, obs_index, obs_value, obs_weight):
    kind = lax.broadcasted_iota(jnp.int32, (1, 4, 4, 128), 1)
    obs = jnp.where(
        kind == 0,
        obs_index.astype(F32)[:, None],
        jnp.where(
            kind == 1,
            obs_value[:, None],
            jnp.where(kind == 2, obs_weight[:, None], obs_count.astype(F32)[:, None, :, None]),
        ),
    )
    which = lax.broadcasted_iota(jnp.int32, (3, 16, 512), 0)
    numbers = jnp.where(which == 0, s, jnp.where(which == 1, z, m))
    sib = swap(state)
    inner_coef, edge_coef, part, halo = own_forecast(state, numbers)
    *inner, halo = sib_forecast(sib, inner_coef, part, halo)
    domains = lax.axis_size("domain")
    pairs = []
    for chip in range(8):
        for d in range(domains - 1):
            pairs.append(((2 * chip + 1) * domains + d, 2 * chip * domains + d + 1))
            pairs.append((2 * chip * domains + d + 1, (2 * chip + 1) * domains + d))
    inner = exchange(inner)
    halo = lax.ppermute(halo, ("member", "domain"), pairs)
    outer = edge_forecast(state, sib, edge_coef, halo)
    first, obs = lax.optimization_barrier((outer[0], obs))
    outer = exchange([first, *outer[1:]])
    obs = [lax.ppermute(obs, "member", pairs) for pairs in obs_pairs()]
    inner = exchange(analysis(False, obs, inner))
    inner_sib = swap(pack(inner, "inner_pack"))
    outer = exchange(analysis(True, obs, outer))
    outer_sib = swap(pack(outer, "edge_pack"))
    return result(inner + outer, [inner_sib, outer_sib])


def solution(mesh):
    placed = (
        P("member", None, "domain", None),
        P("domain", None),
        P("domain", None),
        P("domain", None),
        P(("domain", "member"), None),
        P(("domain", "member"), None, None),
        P(("domain", "member"), None, None),
        P(("domain", "member"), None, None),
    )
    return jax.shard_map(
        shards,
        mesh=mesh,
        in_specs=placed,
        out_specs=P("member", None, "domain", None),
        check_vma=False,
    )
```

```python
import functools
import math

import jax
import jax.numpy as jnp
from jax import lax
from jax.experimental import pallas as pl
from jax.experimental.pallas import tpu as pltpu
from jax.sharding import PartitionSpec as P

ITERS = 6
F32 = jnp.float32
BF16 = jnp.bfloat16


def halves(x):
    high = x.astype(BF16)
    return high, (x - high.astype(F32)).astype(BF16)


def thirds(x):
    high = x.astype(BF16)
    rest = x - high.astype(F32)
    mid = rest.astype(BF16)
    return high, mid, (rest - mid.astype(F32)).astype(BF16)


def dot(a, b):
    return jnp.dot(a, b, preferred_element_type=F32)


ORDER = (3, 5, 2, 6, 4, 1, 7, 0)
BACK = tuple(ORDER.index((8 - d) % 8) for d in ORDER)
PIECE = (2, 8, 16, 256)


def row_picker(rows, first_row):
    out = lax.broadcasted_iota(jnp.int32, (rows * 16, 256), 0)
    src = lax.broadcasted_iota(jnp.int32, (rows * 16, 256), 1)
    row = (out >> 4) + first_row
    hit = jnp.logical_and((src & 15) == row, (src >> 4) == (out & 15))
    return hit.astype(F32).astype(BF16)


def place():
    member = lax.axis_index("member")
    return member >> 1, member & 1


def coefficients(s, z, m):
    return (1.0 - 4.0 * s, s - 0.5 * z, s + 0.5 * z, s - 0.5 * m, s + 0.5 * m)


def step_row(centre, north, south, coef):
    east = pltpu.roll(centre, 511, 1)
    west = pltpu.roll(centre, 1, 1)
    c, e, w, n, so = coef
    return centre * c + east * e + west * w + north * n + south * so


def each_field(work):
    def pair(i, carry):
        for u in range(2):
            work(2 * i + u, u)
        return carry

    lax.fori_loop(0, 4, pair, 0)


def two_steps(rows_at, coef_at, outside, groups, middle, ready):
    coefs = [coef_at(j) for j in range(6)]
    rows = [rows_at(j) for j in range(8)]
    for j in range(6):
        value = step_row(rows[j + 1], rows[j + 2], rows[j], coefs[j])
        middle[j] = value.astype(BF16).astype(F32)
    if outside is not None:
        beyond, at = outside

        @pl.when(beyond)
        def _():
            middle[at] = jnp.zeros((16 * groups, 512), F32)

    for j in range(4):
        value = step_row(middle[j + 1], middle[j + 2], middle[j], coefs[j + 1]).astype(BF16)
        ready[2 * j] = value[:, :256]
        ready[2 * j + 1] = value[:, 256:]


def put_coef(coef, j, numbers):
    for k, value in enumerate(coefficients(*numbers)):
        coef[k, j] = jnp.broadcast_to(value, (8, 512))


def inner_field(pick, flat, c, coef, fields, middle, ready):
    picked = dot(pick[...], flat)
    fields[...] = picked[:128].reshape(8, 16, 512)
    two_steps(
        lambda j: fields[j],
        lambda j: [jnp.concatenate([coef[k, j]] * 2, axis=0) for k in range(5)],
        None,
        1,
        middle,
        ready,
    )
    return picked[128:].astype(BF16).reshape(2, 16, 512)


def own_kernel(own_ref, numbers, inner_coef, edge_coef, part_ref, halo_ref, pick, fields, middle, ready):
    z, c = place()
    pick[:128] = row_picker(8, 2 + 4 * c)
    pick[128:] = row_picker(2, 14 * c)

    def number_rows(row):
        return [numbers[i, pl.ds(row, 1)] for i in range(3)]

    for j in range(6):
        put_coef(inner_coef, j, number_rows(3 + 4 * c + j))
        put_coef(edge_coef, j, number_rows(jnp.clip(12 * c - 1 + j, 0, 15)))
    parts = []
    for value in number_rows(15 * c):
        parts += list(thirds(value))
    parts.append(jnp.zeros((7, 512), BF16))
    halo_ref[8, 0] = jnp.concatenate(parts, axis=0)
    halo_ref[8, 1] = jnp.zeros((16, 512), BF16)

    def one_field(f, u):
        flat = own_ref[:, f].reshape(256, 512)
        halo_ref[f] = inner_field(pick, flat, c, inner_coef, fields.at[u], middle.at[u], ready.at[u])
        for k in range(8):
            part_ref[k, f] = ready[u, (z + ORDER[k]) & 7]

    each_field(one_field)


def sib_kernel(sib_ref, coef, part_ref, own_halo_ref, *rest):
    outs, halo_ref = rest[:8], rest[8]
    pick, fields, middle, ready = rest[9:]
    z, c = place()
    pick[:128] = row_picker(8, 2 + 4 * c)
    pick[128:] = row_picker(2, 14 * c)

    def one_field(f, u):
        flat = sib_ref[:, f].reshape(256, 512)
        halo_ref[f, :, :16] = inner_field(pick, flat, c, coef, fields.at[u], middle.at[u], ready.at[u])
        halo_ref[f, :, 16:] = own_halo_ref[f]
        for k, out_ref in enumerate(outs):
            out_ref[0, f] = part_ref[k, f]
            out_ref[1, f] = ready[u, (z + ORDER[k]) & 7]

    each_field(one_field)
    halo_ref[8, :, :16] = own_halo_ref[8]
    halo_ref[8, :, 16:] = jnp.zeros((2, 16, 512), BF16)


def edge_kernel(own_ref, sib_ref, coef_ref, halo_ref, *rest):
    outs = rest[:8]
    pick, coef, fields, middle, ready = rest[8:]
    z, c = place()
    pick[...] = row_picker(8, 12 * c - 2)
    coef[...] = coef_ref[...]
    part = halo_ref[8, 0].astype(F32)
    put_coef(coef, 5 * c, [part[3 * k : 3 * k + 1] + part[3 * k + 1 : 3 * k + 2] + part[3 * k + 2 : 3 * k + 3] for k in range(3)])
    domain = lax.axis_index("domain")
    outside = jnp.where(c == 0, domain == 0, domain == lax.axis_size("domain") - 1)

    def one_field(f, u):
        fields[u, :, :16] = dot(pick[...], own_ref[:, f].reshape(256, 512)).reshape(8, 16, 512)
        fields[u, :, 16:] = dot(pick[...], sib_ref[:, f].reshape(256, 512)).reshape(8, 16, 512)
        fields[u, pl.ds(6 * c, 2)] = halo_ref[f].astype(F32)
        two_steps(
            lambda j: fields[u, j],
            lambda j: [jnp.concatenate([coef[k, j]] * 4, axis=0) for k in range(5)],
            (outside, 5 * c),
            2,
            middle.at[u],
            ready.at[u],
        )
        for k, out_ref in enumerate(outs):
            out_ref[:, f] = ready[u, (z + ORDER[k]) & 7].reshape(2, 16, 256)

    each_field(one_field)


VMEM = pl.BlockSpec(memory_space=pltpu.VMEM)
ANY = pl.BlockSpec(memory_space=pl.ANY)
LIMIT = pltpu.CompilerParams(vmem_limit_bytes=40 * 1024 * 1024)


def cost(flops, transfer):
    return pl.CostEstimate(flops=flops, bytes_accessed=transfer, transcendentals=0)


def own_forecast(own, numbers):
    shapes = [((5, 6, 8, 512), F32)] * 2 + [((8, 8, 16, 256), BF16), ((9, 2, 16, 512), BF16)]
    return pl.pallas_call(
        own_kernel,
        in_specs=[VMEM] * 2,
        out_specs=[VMEM] * 4,
        out_shape=[jax.ShapeDtypeStruct(*shape) for shape in shapes],
        scratch_shapes=[
            pltpu.VMEM((160, 256), BF16),
            pltpu.VMEM((2, 8, 16, 512), F32),
            pltpu.VMEM((2, 6, 16, 512), F32),
            pltpu.VMEM((2, 8, 16, 256), BF16),
        ],
        compiler_params=LIMIT,
        cost_estimate=cost(300_000_000, 6_000_000),
        name="own_forecast",
    )(own, numbers)


def sib_forecast(sib, coef, part, halo):
    return pl.pallas_call(
        sib_kernel,
        in_specs=[VMEM] * 4,
        out_specs=[VMEM] * 9,
        out_shape=[jax.ShapeDtypeStruct(PIECE, BF16)] * 8 + [jax.ShapeDtypeStruct((9, 2, 32, 512), BF16)],
        scratch_shapes=[
            pltpu.VMEM((160, 256), BF16),
            pltpu.VMEM((2, 8, 16, 512), F32),
            pltpu.VMEM((2, 6, 16, 512), F32),
            pltpu.VMEM((2, 8, 16, 256), BF16),
        ],
        compiler_params=LIMIT,
        cost_estimate=cost(300_000_000, 6_000_000),
        name="sib_forecast",
    )(sib, coef, part, halo)


def edge_forecast(own, sib, coef, halo):
    return pl.pallas_call(
        edge_kernel,
        in_specs=[VMEM] * 4,
        out_specs=[VMEM] * 8,
        out_shape=[jax.ShapeDtypeStruct(PIECE, BF16)] * 8,
        scratch_shapes=[
            pltpu.VMEM((128, 256), BF16),
            pltpu.VMEM((5, 6, 8, 512), F32),
            pltpu.VMEM((2, 8, 32, 512), F32),
            pltpu.VMEM((2, 6, 32, 512), F32),
            pltpu.VMEM((2, 8, 32, 256), BF16),
        ],
        compiler_params=LIMIT,
        cost_estimate=cost(300_000_000, 6_000_000),
        name="edge_forecast",
    )(own, sib, coef, halo)


def left(parts):
    return jnp.concatenate(parts, axis=1)


def right(parts):
    high, low = parts
    top = jnp.concatenate([high, low], axis=1)
    bottom = jnp.concatenate([high, jnp.zeros_like(low)], axis=1)
    return jnp.concatenate([top, bottom], axis=0)


def product(a, b):
    both = dot(a, b)
    return both[:, :128] + both[:, 128:]


def weights_of(patches, members):
    spread = float(members - 1)
    rows = lax.broadcasted_iota(jnp.int32, (128, 128), 0)
    cols = lax.broadcasted_iota(jnp.int32, (128, 128), 1)
    eye = (rows == cols).astype(F32)
    work = []
    for observed, live, value, weight in patches:
        mean = jnp.sum(observed, axis=0, keepdims=True) * (1.0 / members)
        precision_w = weight * live
        root = jnp.sqrt(precision_w)
        scaled = (observed - mean) * root
        work.append({"a": scaled, "v": root * (value - mean)})
    for w in work:
        both = left(halves(w["a"]))
        gram = lax.dot_general(both, both, (((0,), (0,)), ((), ())), preferred_element_type=F32)
        w["g"] = gram[:128, :128] + gram[:128, 128:] + gram[128:, :128]
    for w in work:
        g = w["g"]
        square = jnp.sum(jnp.sum(g * g + (2.0 * spread) * (g * eye), axis=1, keepdims=True), axis=0, keepdims=True)
        scale = jnp.sqrt(square + spread * spread * members)
        inv = 1.0 / scale
        w["scale"], w["inv"] = scale, inv
        w["low"] = spread * inv
        w["y"] = g * inv + w["low"] * eye
        w["z0"] = jnp.ones((1, 1), F32)
    for sweep in range(ITERS):
        last = sweep == ITERS - 1
        for w in work:
            y = w["y"]
            y_parts = halves(y)
            y0 = w["low"] * w["z0"]
            w0 = w["z0"] * y0
            f0 = 1.5 - 0.5 * w0
            if sweep == 0:
                f = 1.5 * eye - 0.5 * y
                fq = -0.5 * eye
                w["next"] = (f, fq, f0, y_parts, None)
            else:
                zz = jnp.concatenate([left(w["z_parts"]), left(w["q_parts"])], axis=0)
                out = product(zz, right(y_parts))
                wq = out[128:] + w["z0"] * (w["low"] * w["q"] + w["z"])
                f = 1.5 * eye - 0.5 * out[:128]
                fq = -0.5 * wq
                w["next"] = (f, fq, f0, y_parts, zz)
        for w in work:
            f, fq, f0, y_parts, zz = w["next"]
            if sweep == 0:
                w["y"] = product(left(y_parts), right(halves(f)))
                w["z"], w["q"] = f, fq
            else:
                rhs = right(halves(f))
                lhs = zz if last else jnp.concatenate([zz, left(y_parts)], axis=0)
                out = product(lhs, rhs)
                w["z"] = out[:128]
                w["q"] = out[128:256] + w["z0"] * fq
                if not last:
                    w["y"] = out[256:]
            w["z0"] = w["z0"] * f0
            if not last:
                w["z_parts"], w["q_parts"] = halves(w["z"]), halves(w["q"])
    for w in work:
        z = right(halves(w["z"]))
        u = jnp.broadcast_to(w["v"], (8, 128))
        u = product(left(halves(u)), z)
        u = product(left(halves(u)), z)
        root = lax.rsqrt(w["scale"])
        w["u"] = u[:1] * root
        w["hat"] = w["a"] * root
        w["c1"] = math.sqrt(spread) * root
    big_rows = lax.broadcasted_iota(jnp.int32, (members, members), 0)
    big_cols = lax.broadcasted_iota(jnp.int32, (members, members), 1)
    big_eye = (big_rows == big_cols).astype(F32)
    result = []
    for w in work:
        hat_high, hat_low = halves(w["hat"])
        t = product(left((hat_high, hat_low)), right(halves(w["q"])))
        t = w["c1"] * t + w["u"]
        t_high, t_low = halves(t)
        nt = (((1,), (1,)), ((), ()))
        full = lax.dot_general(left((t_high, t_low)), left((hat_high, hat_high)), nt, preferred_element_type=F32)
        full = full + lax.dot_general(t_high, hat_low, nt, preferred_element_type=F32)
        result.append((full + (w["c1"] * w["z0"]) * big_eye).astype(BF16))
    return result


def selector(index_row):
    entry = lax.broadcasted_iota(jnp.int32, (1024, 128), 0)
    return (entry == index_row).astype(F32).astype(BF16)


def analysis_kernel(edge, even_ref, odd_ref, *rest):
    pieces, outs, held = rest[:8], rest[8:16], rest[16]
    z, _ = place()
    slot = lax.broadcasted_iota(jnp.int32, (1, 128), 1).astype(F32)
    for k in range(8):
        for g in range(2):
            at = k * 32 + g * 16
            for f in range(8):
                for p in range(2):
                    held[p, at : at + 16, f * 128 : (f + 1) * 128] = pieces[k][g, f, :, p * 128 : (p + 1) * 128]
    patches = []
    for p in range(2):
        patch = pl.ds(2 * (z & 1) + p, 1)
        index, value, weight, count = [
            jnp.where((z & 1) == int(edge), even_ref[0, i, patch], odd_ref[0, i, patch]) for i in range(4)
        ]
        observed = dot(held[p], selector(index.astype(jnp.int32)))
        patches.append((observed, (slot < count).astype(F32), value, weight))
    weights = weights_of(patches, 256)
    for p in range(2):
        for f in range(8):
            x = held[p, :, f * 128 : (f + 1) * 128].astype(F32)
            centre = jnp.sum(x, axis=0, keepdims=True) * (1.0 / 256)
            pert = (x - centre).astype(BF16)
            out = (dot(weights[p], pert) + centre).astype(BF16)
            for k in range(8):
                at = BACK[k] * 32
                outs[k][:, f, :, p * 128 : (p + 1) * 128] = out[at : at + 32].reshape(2, 16, 128)


def analysis(edge, obs, pieces):
    return pl.pallas_call(
        functools.partial(analysis_kernel, edge),
        in_specs=[VMEM] * 10,
        out_specs=[VMEM] * 8,
        out_shape=[jax.ShapeDtypeStruct(PIECE, BF16)] * 8,
        scratch_shapes=[pltpu.VMEM((2, 256, 1024), BF16)],
        compiler_params=LIMIT,
        cost_estimate=cost(2_000_000_000, 6_000_000),
        name="edge_analysis" if edge else "inner_analysis",
    )(*obs, *pieces)


def pack_kernel(*refs):
    z, _ = place()
    for k in range(8):
        refs[8][(z - ORDER[k]) & 7] = refs[k][1]


def pack(pieces, name):
    return pl.pallas_call(
        pack_kernel,
        in_specs=[VMEM] * 8,
        out_specs=VMEM,
        compiler_params=LIMIT,
        out_shape=jax.ShapeDtypeStruct((8, 8, 16, 256), BF16),
        name=name,
    )(*pieces)


def result_kernel(*refs):
    mine, theirs, out_ref, pick, rows, ready, sent = refs[:16], refs[16:18], refs[18], refs[19], refs[20], refs[21], refs[22]
    z, c = place()
    pick[...] = row_picker(16, 0)

    def send(f):
        return pltpu.make_async_copy(ready.at[f], out_ref.at[:, f], sent.at[f])

    def one_field(f, u):
        for chunk in range(2):
            own_base = 12 * c if chunk else 4 + 4 * c
            sib_base = 12 - 12 * c if chunk else 8 - 4 * c
            for k in range(8):
                rows[u, 2 * own_base + ((z - ORDER[k]) & 7)] = mine[8 * chunk + k][0, f]
            for source in range(8):
                rows[u, 2 * sib_base + source] = theirs[chunk][source, f]
        both = rows[u].reshape(16, 2, 16, 256)
        for h in range(2):
            out = dot(pick[...], both[:, h].reshape(256, 256)).astype(BF16)
            ready[f, :, :, h * 256 : (h + 1) * 256] = out.reshape(16, 16, 256)
        send(f).start()

    def finish(f, carry):
        send(f).wait()
        return carry

    each_field(one_field)
    lax.fori_loop(0, 8, finish, 0)


def result(mine, theirs):
    return pl.pallas_call(
        result_kernel,
        in_specs=[VMEM] * 18,
        out_specs=pl.BlockSpec(memory_space=pl.ANY),
        out_shape=jax.ShapeDtypeStruct((16, 8, 16, 512), BF16),
        scratch_shapes=[
            pltpu.VMEM((256, 256), BF16),
            pltpu.VMEM((2, 32, 16, 256), BF16),
            pltpu.VMEM((8, 16, 16, 512), BF16),
            pltpu.SemaphoreType.DMA((8,)),
        ],
        compiler_params=LIMIT,
        name="result",
    )(*mine, *theirs)


def obs_pairs():
    def target(row, odd):
        return 2 * (2 * (row % 4) + odd) + row // 8

    inner = range(4, 12)
    first = [(row, target(row, int(row not in inner))) for row in range(16)]
    return first, [(row, target(row, int(row in inner))) for row in range(16)]


def swap(x):
    return lax.ppermute(x, "member", [(i, i ^ 1) for i in range(16)])


def around(x, distance):
    return lax.ppermute(x, "member", [(i, (i + 2 * distance) % 16) for i in range(16)])


def exchange(pieces):
    return [around(x, d) if d else x for x, d in zip(pieces, ORDER)]


def shards(state, s, z, m, obs_count, obs_index, obs_value, obs_weight):
    kind = lax.broadcasted_iota(jnp.int32, (1, 4, 4, 128), 1)
    obs = jnp.where(
        kind == 0,
        obs_index.astype(F32)[:, None],
        jnp.where(
            kind == 1,
            obs_value[:, None],
            jnp.where(kind == 2, obs_weight[:, None], obs_count.astype(F32)[:, None, :, None]),
        ),
    )
    which = lax.broadcasted_iota(jnp.int32, (3, 16, 512), 0)
    numbers = jnp.where(which == 0, s, jnp.where(which == 1, z, m))
    sib = swap(state)
    inner_coef, edge_coef, part, halo = own_forecast(state, numbers)
    *inner, halo = sib_forecast(sib, inner_coef, part, halo)
    domains = lax.axis_size("domain")
    pairs = []
    for chip in range(8):
        for d in range(domains - 1):
            pairs.append(((2 * chip + 1) * domains + d, 2 * chip * domains + d + 1))
            pairs.append((2 * chip * domains + d + 1, (2 * chip + 1) * domains + d))
    inner = exchange(inner)
    halo = lax.ppermute(halo, ("member", "domain"), pairs)
    outer = edge_forecast(state, sib, edge_coef, halo)
    outer = exchange(outer)
    first, obs = lax.optimization_barrier((inner[0], obs))
    inner = [first, *inner[1:]]
    obs = [lax.ppermute(obs, "member", pairs) for pairs in obs_pairs()]
    inner = exchange(analysis(False, obs, inner))
    inner_sib = swap(pack(inner, "inner_pack"))
    outer = exchange(analysis(True, obs, outer))
    outer_sib = swap(pack(outer, "edge_pack"))
    return result(inner + outer, [inner_sib, outer_sib])


def solution(mesh):
    placed = (
        P("member", None, "domain", None),
        P("domain", None),
        P("domain", None),
        P("domain", None),
        P(("domain", "member"), None),
        P(("domain", "member"), None, None),
        P(("domain", "member"), None, None),
        P(("domain", "member"), None, None),
    )
    return jax.shard_map(
        shards,
        mesh=mesh,
        in_specs=placed,
        out_specs=P("member", None, "domain", None),
        check_vma=False,
    )
```

```python
import functools
import math

import jax
import jax.numpy as jnp
from jax import lax
from jax.experimental import pallas as pl
from jax.experimental.pallas import tpu as pltpu
from jax.sharding import PartitionSpec as P

ITERS = 6
F32 = jnp.float32
BF16 = jnp.bfloat16


def halves(x):
    high = x.astype(BF16)
    return high, (x - high.astype(F32)).astype(BF16)


def thirds(x):
    high = x.astype(BF16)
    rest = x - high.astype(F32)
    mid = rest.astype(BF16)
    return high, mid, (rest - mid.astype(F32)).astype(BF16)


def dot(a, b):
    return jnp.dot(a, b, preferred_element_type=F32)


ORDER = (3, 5, 2, 6, 4, 1, 7, 0)
BACK = tuple(ORDER.index((8 - d) % 8) for d in ORDER)
PIECE = (2, 8, 16, 256)


def row_picker(rows, first_row):
    out = lax.broadcasted_iota(jnp.int32, (rows * 16, 256), 0)
    src = lax.broadcasted_iota(jnp.int32, (rows * 16, 256), 1)
    row = (out >> 4) + first_row
    hit = jnp.logical_and((src & 15) == row, (src >> 4) == (out & 15))
    return hit.astype(F32).astype(BF16)


def place():
    member = lax.axis_index("member")
    return member >> 1, member & 1


def coefficients(s, z, m):
    return (1.0 - 4.0 * s, s - 0.5 * z, s + 0.5 * z, s - 0.5 * m, s + 0.5 * m)


def step_row(centre, north, south, coef):
    east = pltpu.roll(centre, 511, 1)
    west = pltpu.roll(centre, 1, 1)
    c, e, w, n, so = coef
    return centre * c + east * e + west * w + north * n + south * so


def each_field(work):
    def pair(i, carry):
        for u in range(2):
            work(2 * i + u, u)
        return carry

    lax.fori_loop(0, 4, pair, 0)


def two_steps(rows_at, coef_at, outside, groups, middle, ready):
    coefs = [coef_at(j) for j in range(6)]
    rows = [rows_at(j) for j in range(8)]
    for j in range(6):
        value = step_row(rows[j + 1], rows[j + 2], rows[j], coefs[j])
        middle[j] = value.astype(BF16).astype(F32)
    if outside is not None:
        beyond, at = outside

        @pl.when(beyond)
        def _():
            middle[at] = jnp.zeros((16 * groups, 512), F32)

    for j in range(4):
        value = step_row(middle[j + 1], middle[j + 2], middle[j], coefs[j + 1]).astype(BF16)
        ready[2 * j] = value[:, :256]
        ready[2 * j + 1] = value[:, 256:]


def put_coef(coef, j, numbers):
    for k, value in enumerate(coefficients(*numbers)):
        coef[k, j] = jnp.broadcast_to(value, (8, 512))


def inner_field(pick, flat, c, coef, fields, middle, ready):
    picked = dot(pick[...], flat)
    fields[...] = picked[:128].reshape(8, 16, 512)
    two_steps(
        lambda j: fields[j],
        lambda j: [jnp.concatenate([coef[k, j]] * 2, axis=0) for k in range(5)],
        None,
        1,
        middle,
        ready,
    )
    return picked[128:].astype(BF16).reshape(2, 16, 512)


def own_kernel(own_ref, numbers, inner_coef, edge_coef, part_ref, halo_ref, pick, fields, middle, ready):
    z, c = place()
    pick[:128] = row_picker(8, 2 + 4 * c)
    pick[128:] = row_picker(2, 14 * c)

    def number_rows(row):
        return [numbers[i, pl.ds(row, 1)] for i in range(3)]

    for j in range(6):
        put_coef(inner_coef, j, number_rows(3 + 4 * c + j))
        put_coef(edge_coef, j, number_rows(jnp.clip(12 * c - 1 + j, 0, 15)))
    parts = []
    for value in number_rows(15 * c):
        parts += list(thirds(value))
    parts.append(jnp.zeros((7, 512), BF16))
    halo_ref[8, 0] = jnp.concatenate(parts, axis=0)
    halo_ref[8, 1] = jnp.zeros((16, 512), BF16)

    def one_field(f, u):
        flat = own_ref[:, f].reshape(256, 512)
        halo_ref[f] = inner_field(pick, flat, c, inner_coef, fields.at[u], middle.at[u], ready.at[u])
        for k in range(8):
            part_ref[k, f] = ready[u, (z + ORDER[k]) & 7]

    each_field(one_field)


def sib_kernel(sib_ref, coef, part_ref, own_halo_ref, *rest):
    outs, halo_ref = rest[:8], rest[8]
    pick, fields, middle, ready = rest[9:]
    z, c = place()
    pick[:128] = row_picker(8, 2 + 4 * c)
    pick[128:] = row_picker(2, 14 * c)

    def one_field(f, u):
        flat = sib_ref[:, f].reshape(256, 512)
        halo_ref[f, :, :16] = inner_field(pick, flat, c, coef, fields.at[u], middle.at[u], ready.at[u])
        halo_ref[f, :, 16:] = own_halo_ref[f]
        for k, out_ref in enumerate(outs):
            out_ref[0, f] = part_ref[k, f]
            out_ref[1, f] = ready[u, (z + ORDER[k]) & 7]

    each_field(one_field)
    halo_ref[8, :, :16] = own_halo_ref[8]
    halo_ref[8, :, 16:] = jnp.zeros((2, 16, 512), BF16)


def edge_kernel(own_ref, sib_ref, coef_ref, halo_ref, *rest):
    outs = rest[:8]
    pick, coef, fields, middle, ready = rest[8:]
    z, c = place()
    pick[...] = row_picker(8, 12 * c - 2)
    coef[...] = coef_ref[...]
    part = halo_ref[8, 0].astype(F32)
    put_coef(coef, 5 * c, [part[3 * k : 3 * k + 1] + part[3 * k + 1 : 3 * k + 2] + part[3 * k + 2 : 3 * k + 3] for k in range(3)])
    domain = lax.axis_index("domain")
    outside = jnp.where(c == 0, domain == 0, domain == lax.axis_size("domain") - 1)

    def one_field(f, u):
        fields[u, :, :16] = dot(pick[...], own_ref[:, f].reshape(256, 512)).reshape(8, 16, 512)
        fields[u, :, 16:] = dot(pick[...], sib_ref[:, f].reshape(256, 512)).reshape(8, 16, 512)
        fields[u, pl.ds(6 * c, 2)] = halo_ref[f].astype(F32)
        two_steps(
            lambda j: fields[u, j],
            lambda j: [jnp.concatenate([coef[k, j]] * 4, axis=0) for k in range(5)],
            (outside, 5 * c),
            2,
            middle.at[u],
            ready.at[u],
        )
        for k, out_ref in enumerate(outs):
            out_ref[:, f] = ready[u, (z + ORDER[k]) & 7].reshape(2, 16, 256)

    each_field(one_field)


VMEM = pl.BlockSpec(memory_space=pltpu.VMEM)
ANY = pl.BlockSpec(memory_space=pl.ANY)
LIMIT = pltpu.CompilerParams(vmem_limit_bytes=40 * 1024 * 1024)


def cost(flops, transfer):
    return pl.CostEstimate(flops=flops, bytes_accessed=transfer, transcendentals=0)


def own_forecast(own, numbers):
    shapes = [((5, 6, 8, 512), F32)] * 2 + [((8, 8, 16, 256), BF16), ((9, 2, 16, 512), BF16)]
    return pl.pallas_call(
        own_kernel,
        in_specs=[VMEM] * 2,
        out_specs=[VMEM] * 4,
        out_shape=[jax.ShapeDtypeStruct(*shape) for shape in shapes],
        scratch_shapes=[
            pltpu.VMEM((160, 256), BF16),
            pltpu.VMEM((2, 8, 16, 512), F32),
            pltpu.VMEM((2, 6, 16, 512), F32),
            pltpu.VMEM((2, 8, 16, 256), BF16),
        ],
        compiler_params=LIMIT,
        cost_estimate=cost(300_000_000, 6_000_000),
        name="own_forecast",
    )(own, numbers)


def sib_forecast(sib, coef, part, halo):
    return pl.pallas_call(
        sib_kernel,
        in_specs=[VMEM] * 4,
        out_specs=[VMEM] * 9,
        out_shape=[jax.ShapeDtypeStruct(PIECE, BF16)] * 8 + [jax.ShapeDtypeStruct((9, 2, 32, 512), BF16)],
        scratch_shapes=[
            pltpu.VMEM((160, 256), BF16),
            pltpu.VMEM((2, 8, 16, 512), F32),
            pltpu.VMEM((2, 6, 16, 512), F32),
            pltpu.VMEM((2, 8, 16, 256), BF16),
        ],
        compiler_params=LIMIT,
        cost_estimate=cost(300_000_000, 6_000_000),
        name="sib_forecast",
    )(sib, coef, part, halo)


def edge_forecast(own, sib, coef, halo):
    return pl.pallas_call(
        edge_kernel,
        in_specs=[VMEM] * 4,
        out_specs=[VMEM] * 8,
        out_shape=[jax.ShapeDtypeStruct(PIECE, BF16)] * 8,
        scratch_shapes=[
            pltpu.VMEM((128, 256), BF16),
            pltpu.VMEM((5, 6, 8, 512), F32),
            pltpu.VMEM((2, 8, 32, 512), F32),
            pltpu.VMEM((2, 6, 32, 512), F32),
            pltpu.VMEM((2, 8, 32, 256), BF16),
        ],
        compiler_params=LIMIT,
        cost_estimate=cost(300_000_000, 6_000_000),
        name="edge_forecast",
    )(own, sib, coef, halo)


def left(parts):
    return jnp.concatenate(parts, axis=1)


def right(parts):
    high, low = parts
    top = jnp.concatenate([high, low], axis=1)
    bottom = jnp.concatenate([high, jnp.zeros_like(low)], axis=1)
    return jnp.concatenate([top, bottom], axis=0)


def product(a, b):
    both = dot(a, b)
    return both[:, :128] + both[:, 128:]


def weights_of(patches, members):
    spread = float(members - 1)
    rows = lax.broadcasted_iota(jnp.int32, (128, 128), 0)
    cols = lax.broadcasted_iota(jnp.int32, (128, 128), 1)
    eye = (rows == cols).astype(F32)
    work = []
    for observed, live, value, weight in patches:
        mean = jnp.sum(observed, axis=0, keepdims=True) * (1.0 / members)
        precision_w = weight * live
        root = jnp.sqrt(precision_w)
        scaled = (observed - mean) * root
        work.append({"a": scaled, "v": root * (value - mean)})
    for w in work:
        both = left(halves(w["a"]))
        gram = lax.dot_general(both, both, (((0,), (0,)), ((), ())), preferred_element_type=F32)
        w["g"] = gram[:128, :128] + gram[:128, 128:] + gram[128:, :128]
    for w in work:
        g = w["g"]
        square = jnp.sum(jnp.sum(g * g + (2.0 * spread) * (g * eye), axis=1, keepdims=True), axis=0, keepdims=True)
        scale = jnp.sqrt(square + spread * spread * members)
        inv = 1.0 / scale
        w["scale"], w["inv"] = scale, inv
        w["low"] = spread * inv
        w["y"] = g * inv + w["low"] * eye
        w["z0"] = jnp.ones((1, 1), F32)
    for sweep in range(ITERS):
        last = sweep == ITERS - 1
        for w in work:
            y = w["y"]
            y_parts = halves(y)
            y0 = w["low"] * w["z0"]
            w0 = w["z0"] * y0
            f0 = 1.5 - 0.5 * w0
            if sweep == 0:
                f = 1.5 * eye - 0.5 * y
                fq = -0.5 * eye
                w["next"] = (f, fq, f0, y_parts, None)
            else:
                zz = jnp.concatenate([left(w["z_parts"]), left(w["q_parts"])], axis=0)
                out = product(zz, right(y_parts))
                wq = out[128:] + w["z0"] * (w["low"] * w["q"] + w["z"])
                f = 1.5 * eye - 0.5 * out[:128]
                fq = -0.5 * wq
                w["next"] = (f, fq, f0, y_parts, zz)
        for w in work:
            f, fq, f0, y_parts, zz = w["next"]
            if sweep == 0:
                w["y"] = product(left(y_parts), right(halves(f)))
                w["z"], w["q"] = f, fq
            else:
                rhs = right(halves(f))
                lhs = zz if last else jnp.concatenate([zz, left(y_parts)], axis=0)
                out = product(lhs, rhs)
                w["z"] = out[:128]
                w["q"] = out[128:256] + w["z0"] * fq
                if not last:
                    w["y"] = out[256:]
            w["z0"] = w["z0"] * f0
            if not last:
                w["z_parts"], w["q_parts"] = halves(w["z"]), halves(w["q"])
    for w in work:
        z = right(halves(w["z"]))
        u = jnp.broadcast_to(w["v"], (8, 128))
        u = product(left(halves(u)), z)
        u = product(left(halves(u)), z)
        root = lax.rsqrt(w["scale"])
        w["u"] = u[:1] * root
        w["hat"] = w["a"] * root
        w["c1"] = math.sqrt(spread) * root
    big_rows = lax.broadcasted_iota(jnp.int32, (members, members), 0)
    big_cols = lax.broadcasted_iota(jnp.int32, (members, members), 1)
    big_eye = (big_rows == big_cols).astype(F32)
    result = []
    for w in work:
        hat_high, hat_low = halves(w["hat"])
        t = product(left((hat_high, hat_low)), right(halves(w["q"])))
        t = w["c1"] * t + w["u"]
        t_high, t_low = halves(t)
        nt = (((1,), (1,)), ((), ()))
        full = lax.dot_general(left((t_high, t_low)), left((hat_high, hat_high)), nt, preferred_element_type=F32)
        full = full + lax.dot_general(t_high, hat_low, nt, preferred_element_type=F32)
        result.append((full + (w["c1"] * w["z0"]) * big_eye).astype(BF16))
    return result


def selector(index_row):
    entry = lax.broadcasted_iota(jnp.int32, (1024, 128), 0)
    return (entry == index_row).astype(F32).astype(BF16)


def analysis_kernel(edge, even_ref, odd_ref, *rest):
    pieces, outs, held = rest[:8], rest[8:16], rest[16]
    z, _ = place()
    slot = lax.broadcasted_iota(jnp.int32, (1, 128), 1).astype(F32)
    for k in range(8):
        for g in range(2):
            at = k * 32 + g * 16
            for f in range(8):
                for p in range(2):
                    held[p, at : at + 16, f * 128 : (f + 1) * 128] = pieces[k][g, f, :, p * 128 : (p + 1) * 128]
    patches = []
    for p in range(2):
        patch = pl.ds(2 * (z & 1) + p, 1)
        index, value, weight, count = [
            jnp.where((z & 1) == int(edge), even_ref[0, i, patch], odd_ref[0, i, patch]) for i in range(4)
        ]
        observed = dot(held[p], selector(index.astype(jnp.int32)))
        patches.append((observed, (slot < count).astype(F32), value, weight))
    weights = weights_of(patches, 256)
    for p in range(2):
        for f in range(8):
            x = held[p, :, f * 128 : (f + 1) * 128].astype(F32)
            centre = jnp.sum(x, axis=0, keepdims=True) * (1.0 / 256)
            pert = (x - centre).astype(BF16)
            out = (dot(weights[p], pert) + centre).astype(BF16)
            for k in range(8):
                at = BACK[k] * 32
                outs[k][:, f, :, p * 128 : (p + 1) * 128] = out[at : at + 32].reshape(2, 16, 128)


def analysis(edge, obs, pieces):
    return pl.pallas_call(
        functools.partial(analysis_kernel, edge),
        in_specs=[VMEM] * 10,
        out_specs=[VMEM] * 8,
        out_shape=[jax.ShapeDtypeStruct(PIECE, BF16)] * 8,
        scratch_shapes=[pltpu.VMEM((2, 256, 1024), BF16)],
        compiler_params=LIMIT,
        cost_estimate=cost(2_000_000_000, 6_000_000),
        name="edge_analysis" if edge else "inner_analysis",
    )(*obs, *pieces)


def pack_kernel(*refs):
    z, _ = place()
    for k in range(8):
        refs[8][(z - ORDER[k]) & 7] = refs[k][1]


def pack(pieces, name):
    return pl.pallas_call(
        pack_kernel,
        in_specs=[VMEM] * 8,
        out_specs=VMEM,
        compiler_params=LIMIT,
        out_shape=jax.ShapeDtypeStruct((8, 8, 16, 256), BF16),
        name=name,
    )(*pieces)


def result_kernel(*refs):
    mine, theirs, out_ref, pick, rows, ready, sent = refs[:16], refs[16:18], refs[18], refs[19], refs[20], refs[21], refs[22]
    z, c = place()
    pick[...] = row_picker(16, 0)

    def send(f):
        return pltpu.make_async_copy(ready.at[f], out_ref.at[:, f], sent.at[f])

    def one_field(f, u):
        for chunk in range(2):
            own_base = 12 * c if chunk else 4 + 4 * c
            sib_base = 12 - 12 * c if chunk else 8 - 4 * c
            for k in range(8):
                rows[u, 2 * own_base + ((z - ORDER[k]) & 7)] = mine[8 * chunk + k][0, f]
            for source in range(8):
                rows[u, 2 * sib_base + source] = theirs[chunk][source, f]
        both = rows[u].reshape(16, 2, 16, 256)
        for h in range(2):
            out = dot(pick[...], both[:, h].reshape(256, 256)).astype(BF16)
            ready[f, :, :, h * 256 : (h + 1) * 256] = out.reshape(16, 16, 256)
        send(f).start()

    def finish(f, carry):
        send(f).wait()
        return carry

    each_field(one_field)
    lax.fori_loop(0, 8, finish, 0)


def result(mine, theirs):
    return pl.pallas_call(
        result_kernel,
        in_specs=[VMEM] * 18,
        out_specs=pl.BlockSpec(memory_space=pl.ANY),
        out_shape=jax.ShapeDtypeStruct((16, 8, 16, 512), BF16),
        scratch_shapes=[
            pltpu.VMEM((256, 256), BF16),
            pltpu.VMEM((2, 32, 16, 256), BF16),
            pltpu.VMEM((8, 16, 16, 512), BF16),
            pltpu.SemaphoreType.DMA((8,)),
        ],
        compiler_params=LIMIT,
        name="result",
    )(*mine, *theirs)


def obs_pairs():
    def target(row, odd):
        return 2 * (2 * (row % 4) + odd) + row // 8

    inner = range(4, 12)
    first = [(row, target(row, int(row not in inner))) for row in range(16)]
    return first, [(row, target(row, int(row in inner))) for row in range(16)]


def swap(x):
    return lax.ppermute(x, "member", [(i, i ^ 1) for i in range(16)])


def around(x, distance):
    return lax.ppermute(x, "member", [(i, (i + 2 * distance) % 16) for i in range(16)])


def exchange(pieces):
    return [around(x, d) if d else x for x, d in zip(pieces, ORDER)]


def shards(state, s, z, m, obs_count, obs_index, obs_value, obs_weight):
    kind = lax.broadcasted_iota(jnp.int32, (1, 4, 4, 128), 1)
    obs = jnp.where(
        kind == 0,
        obs_index.astype(F32)[:, None],
        jnp.where(
            kind == 1,
            obs_value[:, None],
            jnp.where(kind == 2, obs_weight[:, None], obs_count.astype(F32)[:, None, :, None]),
        ),
    )
    which = lax.broadcasted_iota(jnp.int32, (3, 16, 512), 0)
    numbers = jnp.where(which == 0, s, jnp.where(which == 1, z, m))
    sib = swap(state)
    inner_coef, edge_coef, part, halo = own_forecast(state, numbers)
    *inner, halo = sib_forecast(sib, inner_coef, part, halo)
    domains = lax.axis_size("domain")
    pairs = []
    for chip in range(8):
        for d in range(domains - 1):
            pairs.append(((2 * chip + 1) * domains + d, 2 * chip * domains + d + 1))
            pairs.append((2 * chip * domains + d + 1, (2 * chip + 1) * domains + d))
    inner = exchange(inner)
    halo = lax.ppermute(halo, ("member", "domain"), pairs)
    outer = edge_forecast(state, sib, edge_coef, halo)
    outer = exchange(outer)
    tied, obs = lax.optimization_barrier((inner[4], obs))
    inner[4] = tied
    obs = [lax.ppermute(obs, "member", pairs) for pairs in obs_pairs()]
    inner = exchange(analysis(False, obs, inner))
    inner_sib = swap(pack(inner, "inner_pack"))
    outer = exchange(analysis(True, obs, outer))
    outer_sib = swap(pack(outer, "edge_pack"))
    return result(inner + outer, [inner_sib, outer_sib])


def solution(mesh):
    placed = (
        P("member", None, "domain", None),
        P("domain", None),
        P("domain", None),
        P("domain", None),
        P(("domain", "member"), None),
        P(("domain", "member"), None, None),
        P(("domain", "member"), None, None),
        P(("domain", "member"), None, None),
    )
    return jax.shard_map(
        shards,
        mesh=mesh,
        in_specs=placed,
        out_specs=P("member", None, "domain", None),
        check_vma=False,
    )
```

```python
import functools
import math

import jax
import jax.numpy as jnp
from jax import lax
from jax.experimental import pallas as pl
from jax.experimental.pallas import tpu as pltpu
from jax.sharding import PartitionSpec as P

ITERS = 6
F32 = jnp.float32
BF16 = jnp.bfloat16


def halves(x):
    high = x.astype(BF16)
    return high, (x - high.astype(F32)).astype(BF16)


def thirds(x):
    high = x.astype(BF16)
    rest = x - high.astype(F32)
    mid = rest.astype(BF16)
    return high, mid, (rest - mid.astype(F32)).astype(BF16)


def dot(a, b):
    return jnp.dot(a, b, preferred_element_type=F32)


ORDER = (3, 5, 2, 6, 4, 1, 7, 0)
BACK = tuple(ORDER.index((8 - d) % 8) for d in ORDER)
PIECE = (2, 8, 16, 256)


def row_picker(rows, first_row):
    out = lax.broadcasted_iota(jnp.int32, (rows * 16, 256), 0)
    src = lax.broadcasted_iota(jnp.int32, (rows * 16, 256), 1)
    row = (out >> 4) + first_row
    hit = jnp.logical_and((src & 15) == row, (src >> 4) == (out & 15))
    return hit.astype(F32).astype(BF16)


def place():
    member = lax.axis_index("member")
    return member >> 1, member & 1


def coefficients(s, z, m):
    return (1.0 - 4.0 * s, s - 0.5 * z, s + 0.5 * z, s - 0.5 * m, s + 0.5 * m)


def step_row(centre, north, south, coef):
    east = pltpu.roll(centre, 511, 1)
    west = pltpu.roll(centre, 1, 1)
    c, e, w, n, so = coef
    return centre * c + east * e + west * w + north * n + south * so


def each_field(work):
    def pair(i, carry):
        for u in range(2):
            work(2 * i + u, u)
        return carry

    lax.fori_loop(0, 4, pair, 0)


def two_steps(rows_at, coef_at, outside, groups, middle, ready):
    coefs = [coef_at(j) for j in range(6)]
    rows = [rows_at(j) for j in range(8)]
    for j in range(6):
        value = step_row(rows[j + 1], rows[j + 2], rows[j], coefs[j])
        middle[j] = value.astype(BF16).astype(F32)
    if outside is not None:
        beyond, at = outside

        @pl.when(beyond)
        def _():
            middle[at] = jnp.zeros((16 * groups, 512), F32)

    for j in range(4):
        value = step_row(middle[j + 1], middle[j + 2], middle[j], coefs[j + 1]).astype(BF16)
        ready[2 * j] = value[:, :256]
        ready[2 * j + 1] = value[:, 256:]


def put_coef(coef, j, numbers):
    for k, value in enumerate(coefficients(*numbers)):
        coef[k, j] = jnp.broadcast_to(value, (8, 512))


def inner_field(pick, flat, c, coef, fields, middle, ready):
    picked = dot(pick[...], flat)
    fields[...] = picked[:128].reshape(8, 16, 512)
    two_steps(
        lambda j: fields[j],
        lambda j: [jnp.concatenate([coef[k, j]] * 2, axis=0) for k in range(5)],
        None,
        1,
        middle,
        ready,
    )
    return picked[128:].astype(BF16).reshape(2, 16, 512)


def own_kernel(own_ref, numbers, inner_coef, edge_coef, part_ref, halo_ref, pick, fields, middle, ready):
    z, c = place()
    pick[:128] = row_picker(8, 2 + 4 * c)
    pick[128:] = row_picker(2, 14 * c)

    def number_rows(row):
        return [numbers[i, pl.ds(row, 1)] for i in range(3)]

    for j in range(6):
        put_coef(inner_coef, j, number_rows(3 + 4 * c + j))
        put_coef(edge_coef, j, number_rows(jnp.clip(12 * c - 1 + j, 0, 15)))
    parts = []
    for value in number_rows(15 * c):
        parts += list(thirds(value))
    parts.append(jnp.zeros((7, 512), BF16))
    halo_ref[8, 0] = jnp.concatenate(parts, axis=0)
    halo_ref[8, 1] = jnp.zeros((16, 512), BF16)

    def one_field(f, u):
        flat = own_ref[:, f].reshape(256, 512)
        halo_ref[f] = inner_field(pick, flat, c, inner_coef, fields.at[u], middle.at[u], ready.at[u])
        for k in range(8):
            part_ref[k, f] = ready[u, (z + ORDER[k]) & 7]

    each_field(one_field)


def sib_kernel(sib_ref, coef, part_ref, own_halo_ref, *rest):
    outs, halo_ref = rest[:8], rest[8]
    pick, fields, middle, ready = rest[9:]
    z, c = place()
    pick[:128] = row_picker(8, 2 + 4 * c)
    pick[128:] = row_picker(2, 14 * c)

    def one_field(f, u):
        flat = sib_ref[:, f].reshape(256, 512)
        halo_ref[f, :, :16] = inner_field(pick, flat, c, coef, fields.at[u], middle.at[u], ready.at[u])
        halo_ref[f, :, 16:] = own_halo_ref[f]
        for k, out_ref in enumerate(outs):
            out_ref[0, f] = part_ref[k, f]
            out_ref[1, f] = ready[u, (z + ORDER[k]) & 7]

    each_field(one_field)
    halo_ref[8, :, :16] = own_halo_ref[8]
    halo_ref[8, :, 16:] = jnp.zeros((2, 16, 512), BF16)


def edge_kernel(own_ref, sib_ref, coef_ref, halo_ref, *rest):
    outs = rest[:8]
    pick, coef, fields, middle, ready = rest[8:]
    z, c = place()
    pick[...] = row_picker(8, 12 * c - 2)
    coef[...] = coef_ref[...]
    part = halo_ref[8, 0].astype(F32)
    put_coef(coef, 5 * c, [part[3 * k : 3 * k + 1] + part[3 * k + 1 : 3 * k + 2] + part[3 * k + 2 : 3 * k + 3] for k in range(3)])
    domain = lax.axis_index("domain")
    outside = jnp.where(c == 0, domain == 0, domain == lax.axis_size("domain") - 1)

    def one_field(f, u):
        fields[u, :, :16] = dot(pick[...], own_ref[:, f].reshape(256, 512)).reshape(8, 16, 512)
        fields[u, :, 16:] = dot(pick[...], sib_ref[:, f].reshape(256, 512)).reshape(8, 16, 512)
        fields[u, pl.ds(6 * c, 2)] = halo_ref[f].astype(F32)
        two_steps(
            lambda j: fields[u, j],
            lambda j: [jnp.concatenate([coef[k, j]] * 4, axis=0) for k in range(5)],
            (outside, 5 * c),
            2,
            middle.at[u],
            ready.at[u],
        )
        for k, out_ref in enumerate(outs):
            out_ref[:, f] = ready[u, (z + ORDER[k]) & 7].reshape(2, 16, 256)

    each_field(one_field)


VMEM = pl.BlockSpec(memory_space=pltpu.VMEM)
ANY = pl.BlockSpec(memory_space=pl.ANY)
LIMIT = pltpu.CompilerParams(vmem_limit_bytes=40 * 1024 * 1024)


def cost(flops, transfer):
    return pl.CostEstimate(flops=flops, bytes_accessed=transfer, transcendentals=0)


def own_forecast(own, numbers):
    shapes = [((5, 6, 8, 512), F32)] * 2 + [((8, 8, 16, 256), BF16), ((9, 2, 16, 512), BF16)]
    return pl.pallas_call(
        own_kernel,
        in_specs=[VMEM] * 2,
        out_specs=[VMEM] * 4,
        out_shape=[jax.ShapeDtypeStruct(*shape) for shape in shapes],
        scratch_shapes=[
            pltpu.VMEM((160, 256), BF16),
            pltpu.VMEM((2, 8, 16, 512), F32),
            pltpu.VMEM((2, 6, 16, 512), F32),
            pltpu.VMEM((2, 8, 16, 256), BF16),
        ],
        compiler_params=LIMIT,
        cost_estimate=cost(3_000_000_000, 6_000_000),
        name="own_forecast",
    )(own, numbers)


def sib_forecast(sib, coef, part, halo):
    return pl.pallas_call(
        sib_kernel,
        in_specs=[VMEM] * 4,
        out_specs=[VMEM] * 9,
        out_shape=[jax.ShapeDtypeStruct(PIECE, BF16)] * 8 + [jax.ShapeDtypeStruct((9, 2, 32, 512), BF16)],
        scratch_shapes=[
            pltpu.VMEM((160, 256), BF16),
            pltpu.VMEM((2, 8, 16, 512), F32),
            pltpu.VMEM((2, 6, 16, 512), F32),
            pltpu.VMEM((2, 8, 16, 256), BF16),
        ],
        compiler_params=LIMIT,
        cost_estimate=cost(3_000_000_000, 6_000_000),
        name="sib_forecast",
    )(sib, coef, part, halo)


def edge_forecast(own, sib, coef, halo):
    return pl.pallas_call(
        edge_kernel,
        in_specs=[VMEM] * 4,
        out_specs=[VMEM] * 8,
        out_shape=[jax.ShapeDtypeStruct(PIECE, BF16)] * 8,
        scratch_shapes=[
            pltpu.VMEM((128, 256), BF16),
            pltpu.VMEM((5, 6, 8, 512), F32),
            pltpu.VMEM((2, 8, 32, 512), F32),
            pltpu.VMEM((2, 6, 32, 512), F32),
            pltpu.VMEM((2, 8, 32, 256), BF16),
        ],
        compiler_params=LIMIT,
        cost_estimate=cost(3_000_000_000, 6_000_000),
        name="edge_forecast",
    )(own, sib, coef, halo)


def left(parts):
    return jnp.concatenate(parts, axis=1)


def right(parts):
    high, low = parts
    top = jnp.concatenate([high, low], axis=1)
    bottom = jnp.concatenate([high, jnp.zeros_like(low)], axis=1)
    return jnp.concatenate([top, bottom], axis=0)


def product(a, b):
    both = dot(a, b)
    return both[:, :128] + both[:, 128:]


def weights_of(patches, members):
    spread = float(members - 1)
    rows = lax.broadcasted_iota(jnp.int32, (128, 128), 0)
    cols = lax.broadcasted_iota(jnp.int32, (128, 128), 1)
    eye = (rows == cols).astype(F32)
    work = []
    for observed, live, value, weight in patches:
        mean = jnp.sum(observed, axis=0, keepdims=True) * (1.0 / members)
        precision_w = weight * live
        root = jnp.sqrt(precision_w)
        scaled = (observed - mean) * root
        work.append({"a": scaled, "v": root * (value - mean)})
    for w in work:
        both = left(halves(w["a"]))
        gram = lax.dot_general(both, both, (((0,), (0,)), ((), ())), preferred_element_type=F32)
        w["g"] = gram[:128, :128] + gram[:128, 128:] + gram[128:, :128]
    for w in work:
        g = w["g"]
        square = jnp.sum(jnp.sum(g * g + (2.0 * spread) * (g * eye), axis=1, keepdims=True), axis=0, keepdims=True)
        scale = jnp.sqrt(square + spread * spread * members)
        inv = 1.0 / scale
        w["scale"], w["inv"] = scale, inv
        w["low"] = spread * inv
        w["y"] = g * inv + w["low"] * eye
        w["z0"] = jnp.ones((1, 1), F32)
    for sweep in range(ITERS):
        last = sweep == ITERS - 1
        for w in work:
            y = w["y"]
            y_parts = halves(y)
            y0 = w["low"] * w["z0"]
            w0 = w["z0"] * y0
            f0 = 1.5 - 0.5 * w0
            if sweep == 0:
                f = 1.5 * eye - 0.5 * y
                fq = -0.5 * eye
                w["next"] = (f, fq, f0, y_parts, None)
            else:
                zz = jnp.concatenate([left(w["z_parts"]), left(w["q_parts"])], axis=0)
                out = product(zz, right(y_parts))
                wq = out[128:] + w["z0"] * (w["low"] * w["q"] + w["z"])
                f = 1.5 * eye - 0.5 * out[:128]
                fq = -0.5 * wq
                w["next"] = (f, fq, f0, y_parts, zz)
        for w in work:
            f, fq, f0, y_parts, zz = w["next"]
            if sweep == 0:
                w["y"] = product(left(y_parts), right(halves(f)))
                w["z"], w["q"] = f, fq
            else:
                rhs = right(halves(f))
                lhs = zz if last else jnp.concatenate([zz, left(y_parts)], axis=0)
                out = product(lhs, rhs)
                w["z"] = out[:128]
                w["q"] = out[128:256] + w["z0"] * fq
                if not last:
                    w["y"] = out[256:]
            w["z0"] = w["z0"] * f0
            if not last:
                w["z_parts"], w["q_parts"] = halves(w["z"]), halves(w["q"])
    for w in work:
        z = right(halves(w["z"]))
        u = jnp.broadcast_to(w["v"], (8, 128))
        u = product(left(halves(u)), z)
        u = product(left(halves(u)), z)
        root = lax.rsqrt(w["scale"])
        w["u"] = u[:1] * root
        w["hat"] = w["a"] * root
        w["c1"] = math.sqrt(spread) * root
    big_rows = lax.broadcasted_iota(jnp.int32, (members, members), 0)
    big_cols = lax.broadcasted_iota(jnp.int32, (members, members), 1)
    big_eye = (big_rows == big_cols).astype(F32)
    result = []
    for w in work:
        hat_high, hat_low = halves(w["hat"])
        t = product(left((hat_high, hat_low)), right(halves(w["q"])))
        t = w["c1"] * t + w["u"]
        t_high, t_low = halves(t)
        nt = (((1,), (1,)), ((), ()))
        full = lax.dot_general(left((t_high, t_low)), left((hat_high, hat_high)), nt, preferred_element_type=F32)
        full = full + lax.dot_general(t_high, hat_low, nt, preferred_element_type=F32)
        result.append((full + (w["c1"] * w["z0"]) * big_eye).astype(BF16))
    return result


def selector(index_row):
    entry = lax.broadcasted_iota(jnp.int32, (1024, 128), 0)
    return (entry == index_row).astype(F32).astype(BF16)


def analysis_kernel(edge, even_ref, odd_ref, *rest):
    pieces, outs, held = rest[:8], rest[8:16], rest[16]
    z, _ = place()
    slot = lax.broadcasted_iota(jnp.int32, (1, 128), 1).astype(F32)
    for k in range(8):
        for g in range(2):
            at = k * 32 + g * 16
            for f in range(8):
                for p in range(2):
                    held[p, at : at + 16, f * 128 : (f + 1) * 128] = pieces[k][g, f, :, p * 128 : (p + 1) * 128]
    patches = []
    for p in range(2):
        patch = pl.ds(2 * (z & 1) + p, 1)
        index, value, weight, count = [
            jnp.where((z & 1) == int(edge), even_ref[0, i, patch], odd_ref[0, i, patch]) for i in range(4)
        ]
        observed = dot(held[p], selector(index.astype(jnp.int32)))
        patches.append((observed, (slot < count).astype(F32), value, weight))
    weights = weights_of(patches, 256)
    for p in range(2):
        for f in range(8):
            x = held[p, :, f * 128 : (f + 1) * 128].astype(F32)
            centre = jnp.sum(x, axis=0, keepdims=True) * (1.0 / 256)
            pert = (x - centre).astype(BF16)
            out = (dot(weights[p], pert) + centre).astype(BF16)
            for k in range(8):
                at = BACK[k] * 32
                outs[k][:, f, :, p * 128 : (p + 1) * 128] = out[at : at + 32].reshape(2, 16, 128)


def analysis(edge, obs, pieces):
    return pl.pallas_call(
        functools.partial(analysis_kernel, edge),
        in_specs=[VMEM] * 10,
        out_specs=[VMEM] * 8,
        out_shape=[jax.ShapeDtypeStruct(PIECE, BF16)] * 8,
        scratch_shapes=[pltpu.VMEM((2, 256, 1024), BF16)],
        compiler_params=LIMIT,
        cost_estimate=cost(5_000_000_000, 6_000_000),
        name="edge_analysis" if edge else "inner_analysis",
    )(*obs, *pieces)


def pack_kernel(*refs):
    z, _ = place()
    for k in range(8):
        refs[8][(z - ORDER[k]) & 7] = refs[k][1]


def pack(pieces, name):
    return pl.pallas_call(
        pack_kernel,
        in_specs=[VMEM] * 8,
        out_specs=VMEM,
        compiler_params=LIMIT,
        out_shape=jax.ShapeDtypeStruct((8, 8, 16, 256), BF16),
        name=name,
    )(*pieces)


def result_kernel(*refs):
    mine, theirs, out_ref, pick, rows, ready, sent = refs[:16], refs[16:18], refs[18], refs[19], refs[20], refs[21], refs[22]
    z, c = place()
    pick[...] = row_picker(16, 0)

    def send(f):
        return pltpu.make_async_copy(ready.at[f], out_ref.at[:, f], sent.at[f])

    def one_field(f, u):
        for chunk in range(2):
            own_base = 12 * c if chunk else 4 + 4 * c
            sib_base = 12 - 12 * c if chunk else 8 - 4 * c
            for k in range(8):
                rows[u, 2 * own_base + ((z - ORDER[k]) & 7)] = mine[8 * chunk + k][0, f]
            for source in range(8):
                rows[u, 2 * sib_base + source] = theirs[chunk][source, f]
        both = rows[u].reshape(16, 2, 16, 256)
        for h in range(2):
            out = dot(pick[...], both[:, h].reshape(256, 256)).astype(BF16)
            ready[f, :, :, h * 256 : (h + 1) * 256] = out.reshape(16, 16, 256)
        send(f).start()

    def finish(f, carry):
        send(f).wait()
        return carry

    each_field(one_field)
    lax.fori_loop(0, 8, finish, 0)


def result(mine, theirs):
    return pl.pallas_call(
        result_kernel,
        in_specs=[VMEM] * 18,
        out_specs=pl.BlockSpec(memory_space=pl.ANY),
        out_shape=jax.ShapeDtypeStruct((16, 8, 16, 512), BF16),
        scratch_shapes=[
            pltpu.VMEM((256, 256), BF16),
            pltpu.VMEM((2, 32, 16, 256), BF16),
            pltpu.VMEM((8, 16, 16, 512), BF16),
            pltpu.SemaphoreType.DMA((8,)),
        ],
        compiler_params=LIMIT,
        name="result",
    )(*mine, *theirs)


def obs_pairs():
    def target(row, odd):
        return 2 * (2 * (row % 4) + odd) + row // 8

    inner = range(4, 12)
    first = [(row, target(row, int(row not in inner))) for row in range(16)]
    return first, [(row, target(row, int(row in inner))) for row in range(16)]


def swap(x):
    return lax.ppermute(x, "member", [(i, i ^ 1) for i in range(16)])


def around(x, distance):
    return lax.ppermute(x, "member", [(i, (i + 2 * distance) % 16) for i in range(16)])


def exchange(pieces):
    return [around(x, d) if d else x for x, d in zip(pieces, ORDER)]


def shards(state, s, z, m, obs_count, obs_index, obs_value, obs_weight):
    kind = lax.broadcasted_iota(jnp.int32, (1, 4, 4, 128), 1)
    obs = jnp.where(
        kind == 0,
        obs_index.astype(F32)[:, None],
        jnp.where(
            kind == 1,
            obs_value[:, None],
            jnp.where(kind == 2, obs_weight[:, None], obs_count.astype(F32)[:, None, :, None]),
        ),
    )
    which = lax.broadcasted_iota(jnp.int32, (3, 16, 512), 0)
    numbers = jnp.where(which == 0, s, jnp.where(which == 1, z, m))
    sib = swap(state)
    inner_coef, edge_coef, part, halo = own_forecast(state, numbers)
    *inner, halo = sib_forecast(sib, inner_coef, part, halo)
    domains = lax.axis_size("domain")
    pairs = []
    for chip in range(8):
        for d in range(domains - 1):
            pairs.append(((2 * chip + 1) * domains + d, 2 * chip * domains + d + 1))
            pairs.append((2 * chip * domains + d + 1, (2 * chip + 1) * domains + d))
    inner = exchange(inner)
    halo = lax.ppermute(halo, ("member", "domain"), pairs)
    outer = edge_forecast(state, sib, edge_coef, halo)
    outer = exchange(outer)
    tied, obs = lax.optimization_barrier((inner[4], obs))
    inner[4] = tied
    obs = [lax.ppermute(obs, "member", pairs) for pairs in obs_pairs()]
    inner = exchange(analysis(False, obs, inner))
    inner_sib = swap(pack(inner, "inner_pack"))
    outer = exchange(analysis(True, obs, outer))
    outer_sib = swap(pack(outer, "edge_pack"))
    return result(inner + outer, [inner_sib, outer_sib])


def solution(mesh):
    placed = (
        P("member", None, "domain", None),
        P("domain", None),
        P("domain", None),
        P("domain", None),
        P(("domain", "member"), None),
        P(("domain", "member"), None, None),
        P(("domain", "member"), None, None),
        P(("domain", "member"), None, None),
    )
    return jax.shard_map(
        shards,
        mesh=mesh,
        in_specs=placed,
        out_specs=P("member", None, "domain", None),
        check_vma=False,
    )
```
